1024 devices in a mesh: rep: 64 (over x, y_lo, core), fsdp: 16 (over y_hi, z).
Axes of the slice: x: 8, y: 8 (y_hi: 2, y_lo: 4; y = y_hi * 4 + y_lo), z: 8, core: 2. Of those that a mesh axis runs over, the one named last changes fastest.
Arguments:
- tokens: bfloat16 [131072, 5120], P(('rep', 'fsdp')), may hold values from -6 to 6
- momentum: float32 [64, 512, 5120], P('rep', 'fsdp'), may hold values from -6 to 6
- gradient: bfloat16 [64, 512, 5120], P('rep', 'fsdp'), may hold values from -6 to 6
- weight: bfloat16 [512, 5120], P('fsdp'), may hold values from -0.078125 to 0.078125
- kept_index: int32 [512, 80, 8], P('fsdp'), may hold values from 0 to 63, all different within a row
Outputs:
- new_weight: bfloat16 [512, 5120], P('fsdp')
- new_momentum: float32 [64, 512, 5120], P('rep', 'fsdp')
- projected: bfloat16 [131072, 512], P(('rep', 'fsdp'))
The draws below stay inside these ranges and needn't reach their ends.
Inputs may be any that keep to these rules, and one draw needn't show every extreme that they name: `kept_index`: the 8 entries of each block are distinct frequencies.
All inputs are finite; a program needn't handle non-finite values.
Results may differ from the reference program's by a relative error of at most 0.005.
Values may be sent and summed in bfloat16 or wider, within the bound.
No kernel may reach another device: no remote copies, remote signals or barrier semaphores. Data moves between devices by JAX's collectives and lax.ppermute only.
A program may use at most 64 MiB of HBM per device.

```python
import jax
import jax.numpy as jnp
from jax import lax

D = 5120
GROUP = 64
KEEP = 8
FFW = 512
REP = 64
TOKENS = 131072


def block_scale(key, dims, pieces, smallest, high):
    gain = 1.0
    for dim, parts in pieces:
        draws = jax.random.uniform(jax.random.fold_in(jax.random.fold_in(key, 6), dim), (parts,), jnp.float32, smallest / len(pieces), high / len(pieces))
        gain = gain * jnp.repeat(jnp.exp(draws), dims[dim] // parts).reshape((-1,) + (1,) * (len(dims) - 1 - dim))
    return gain


def picks_of(stream_key, rows, count, top, lift):
    ranking = jax.random.permutation(jax.random.fold_in(stream_key, 1), count)
    pull = ranking
    for power in range(3):
        pull = pull * pull // count
    pull = pull * lift // count
    tickets = jax.random.randint(jax.random.fold_in(stream_key, 2), (rows, count), 0, 4096) + pull
    sure = jax.random.permutation(jax.random.fold_in(stream_key, 3), rows)[jnp.arange(count) % rows]
    tickets = jnp.where(jnp.arange(rows)[:, None] == sure[None, :], 1 << 14, tickets)
    priority = tickets * count + jnp.arange(count)
    return lax.top_k(priority.astype(jnp.int32), top)[1].astype(jnp.int32)


def noise(rng, dims, scale, limit, shards=(), kind=jnp.bfloat16):
    entries = scale * jax.random.normal(rng, dims, jnp.float32)
    if shards:
        entries = entries * block_scale(rng, dims, shards, -0.22, 0.18)
    return jnp.clip(entries, -limit, limit).astype(kind)


def setup_inputs(seed: int = 0) -> dict:
    key_of = jax.random.split(jax.random.key(seed), 6)
    tokens = noise(key_of[0], (TOKENS, D), 1.0, 6.0, ((0, 1024),))
    momentum = noise(key_of[1], (REP, FFW, D), 1.0, 6.0, ((0, 64), (1, 16)), jnp.float32)
    gradient = noise(key_of[2], (REP, FFW, D), 1.0, 6.0, ((0, 64), (1, 16)))
    weight = noise(key_of[3], (FFW, D), D ** -0.5, 0.078125, ((0, 16),))
    kept_index = picks_of(key_of[4], FFW * (D // GROUP), GROUP, KEEP, 0).reshape((FFW, D // GROUP, KEEP))
    return dict(tokens=tokens, momentum=momentum, gradient=gradient, weight=weight, kept_index=kept_index)


step_size = 0.01
decay_rate = 0.1

def cosine_table():
    frequency = jnp.arange(GROUP, dtype=jnp.float32)[:, None]
    position = jnp.arange(GROUP, dtype=jnp.float32)[None, :]
    factor = jnp.where(frequency == 0.0, jnp.sqrt(1.0 / GROUP), jnp.sqrt(2.0 / GROUP)).astype(jnp.float32)
    return (factor * jnp.cos(jnp.pi * (position + 0.5) * frequency / GROUP)).astype(jnp.float32)

def reference(tokens, momentum, gradient, weight, kept_index):
    highest = lax.Precision.HIGHEST
    nblocks = D // GROUP
    accum = 0.9 * momentum + gradient.astype(jnp.float32)
    blocks = accum.reshape(REP, FFW, nblocks, GROUP)
    onehot = (kept_index[..., None] == jnp.arange(GROUP, dtype=jnp.int32)).astype(jnp.float32)
    basis_rows = jnp.einsum('fckj,jn->fckn', onehot, cosine_table(), precision=highest)
    kept = jnp.einsum('rfcn,fckn->rfck', blocks, basis_rows, precision=highest)
    sent_part = jnp.einsum('rfck,fckn->rfcn', kept, basis_rows, precision=highest)
    new_momentum = (blocks - sent_part).reshape(REP, FFW, D)
    total = lax.optimization_barrier(jnp.sum(kept, axis=0))
    dense = jnp.einsum('fck,fckn->fcn', total, basis_rows, precision=highest)
    direction = dense / jnp.sqrt(lax.optimization_barrier(jnp.mean(dense * dense, axis=-1, keepdims=True)) + 1e-06)
    new_weight = (weight.astype(jnp.float32) * (1.0 - step_size * decay_rate) - step_size * direction.reshape(FFW, D)).astype(jnp.bfloat16)
    projected = lax.dot_general(tokens, new_weight, (((1,), (1,)), ((), ())), preferred_element_type=jnp.float32).astype(jnp.bfloat16)
    return (new_weight, new_momentum, projected)
```

```python
import functools
import math

import jax
import jax.numpy as jnp
import numpy as np
from jax import lax
from jax.experimental import pallas as pl
from jax.experimental.pallas import tpu as pltpu
from jax.sharding import Mesh
from jax.sharding import PartitionSpec as P

GROUP = 64
KEEP = 8
LANES = 128
STACK = 4
HIGHEST = lax.Precision.HIGHEST
STEP = 0.01
DECAY = 0.1
AXES = ("x", "ylo", "core", "yhi", "z")
F32 = jnp.float32
BF16 = jnp.bfloat16
NT = (((1,), (1,)), ((), ()))
NN = (((1,), (0,)), ((), ()))
TN = (((0,), (0,)), ((), ()))


def basis_pair():
    k = np.arange(GROUP)[:, None]
    n = np.arange(GROUP)[None, :]
    scale = np.where(k == 0, math.sqrt(1.0 / GROUP), math.sqrt(2.0 / GROUP))
    table = scale * np.cos(np.pi * (n + 0.5) * k / GROUP)
    return np.kron(np.eye(2), table).astype(np.float32)


def call(kernel, out_shape, args, flops, **kw):
    size = sum(a.size * a.dtype.itemsize for a in args)
    return pl.pallas_call(
        kernel,
        out_shape=out_shape,
        compiler_params=pltpu.CompilerParams(vmem_limit_bytes=48 * 1024 * 1024),
        cost_estimate=pl.CostEstimate(flops=flops, bytes_accessed=size, transcendentals=0),
        **kw,
    )(*args)


def to_all(x, axes, parts):
    copies = lax.optimization_barrier(jnp.broadcast_to(x[None], (parts,) + x.shape))
    return lax.all_to_all(copies, axes, 0, 0, tiled=True)


def regroup(blocks, rows, target):
    fold = LANES // rows
    lane = lax.broadcasted_iota(jnp.int32, blocks[0].shape, 1) // rows
    merged = None
    for b in range(fold):
        moved = blocks[b]
        if b != target:
            moved = pltpu.roll(moved, ((b - target) % fold) * rows, axis=1)
        merged = moved if merged is None else jnp.where(lane == b, moved, merged)
    return merged


def local_kernel(cores, mom, grad, idx, b2, kept, idx_out, new_mom, kept_wide, idx_wide):
    rows = mom.shape[0]
    total_units = idx.shape[0] // KEEP
    units = total_units // cores
    deep = kept_wide.shape[1]
    table = b2[...]
    freq = lax.broadcasted_iota(jnp.int32, (GROUP, LANES), 0)
    kept_wide[...] = jnp.zeros_like(kept_wide)
    idx_wide[...] = jnp.zeros_like(idx_wide)
    for g in range(total_units // 2):
        tiles = []
        for t in range(STACK):
            cols = pl.ds((STACK * g + t) * LANES, LANES)
            tiles.append(0.9 * mom[:, cols] + grad[:, cols].astype(F32))
        block = jnp.concatenate(tiles, axis=0)
        spec = lax.dot_general(table, block, NT, precision=HIGHEST, preferred_element_type=F32)
        parts = []
        for c2 in range(2):
            whole = 2 * g + c2
            core, u = whole // units, whole % units
            half = spec[c2 * GROUP : (c2 + 1) * GROUP]
            sent = jnp.zeros_like(half)
            for j in range(KEEP):
                line = j * total_units + whole
                row = idx[line : line + 1, :]
                one = jnp.where(freq == row, half, 0.0)
                at = core * KEEP + j
                kept_wide[u % STACK, u // STACK, at : at + 1, :] = jnp.sum(one, axis=0, keepdims=True)
                idx_wide[u % STACK, u // STACK, at : at + 1, :] = row.astype(F32)
                sent = sent + one
            parts.append(sent)
        sent = lax.dot_general(jnp.concatenate(parts, axis=0), table, TN, precision=HIGHEST, preferred_element_type=F32)
        rest = block - sent
        for t in range(STACK):
            new_mom[:, pl.ds((STACK * g + t) * LANES, LANES)] = rest[t * rows : (t + 1) * rows]
    both = cores * KEEP
    for ur in range(deep):
        for t in range(STACK):
            lines = pl.ds(t * both * deep + ur, both, stride=deep)
            kept[lines, :] = regroup([kept_wide[b, ur] for b in range(STACK)], rows, t)
            idx_out[lines, :] = regroup([idx_wide[b, ur] for b in range(STACK)], rows, t)


def weight_kernel(tot, idx, b2, old, new, tot_wide, idx_wide):
    rows, width = old.shape
    deep = tot.shape[0] // (STACK * KEEP)
    span = KEEP * deep
    for source, wide in ((tot, tot_wide), (idx, idx_wide)):
        for b in range(STACK):
            wide[b] = regroup([source[t * span : (t + 1) * span, :] for t in range(STACK)], rows, b)
    freq = lax.broadcasted_iota(jnp.int32, (GROUP, LANES), 0)
    for g in range(width // (STACK * LANES)):
        parts = []
        for c2 in range(2):
            u = 2 * g + c2
            lines = pl.ds(u // STACK, KEEP, stride=deep)
            value = tot_wide[u % STACK, lines, :]
            where = idx_wide[u % STACK, lines, :].astype(jnp.int32)
            power = jnp.sum(value * value, axis=0, keepdims=True)
            value = value * lax.rsqrt(power / GROUP + 1e-06)
            spec = jnp.zeros((GROUP, LANES), F32)
            for j in range(KEEP):
                spec = jnp.where(freq == where[j : j + 1], value[j : j + 1], spec)
            parts.append(spec)
        direction = lax.dot_general(
            jnp.concatenate(parts, axis=0), b2[...], TN, precision=HIGHEST, preferred_element_type=F32
        )
        for t in range(STACK):
            cols = pl.ds((STACK * g + t) * LANES, LANES)
            kept_part = old[:, cols].astype(F32) * (1.0 - STEP * DECAY)
            new[:, cols] = (kept_part - STEP * direction[t * rows : (t + 1) * rows]).astype(BF16)


def tokens_kernel(mine, theirs, high, low, out):
    batch = mine.shape[0]
    for t in range(mine.shape[1] // LANES):
        cols = pl.ds(t * LANES, LANES)
        x = jnp.concatenate([mine[:, cols], theirs[:, cols]], axis=0)
        y = lax.dot_general(x, high[...], NT, preferred_element_type=F32)
        y = y + lax.dot_general(x, low[...], NT, preferred_element_type=F32)
        out[:, cols] = y.astype(BF16)


def direction_kernel(rows, units, both, tokens, out, vals, freqs, spec):
    shards = both.shape[0]
    lines = both.shape[1] // 2
    deep = lines // (STACK * KEEP)
    fold = LANES // rows
    for q in range(shards // fold):
        blocks = [both[fold * q + f].astype(F32) for f in range(fold)]
        for b in range(STACK):
            vals[b, q] = regroup([x[:lines] for x in blocks], rows, b)
            freqs[b, q] = regroup([x[lines:] for x in blocks], rows, b).astype(jnp.int32)
    freq = lax.broadcasted_iota(jnp.int32, (GROUP, LANES), 0)
    depth = 2 * STACK * GROUP
    for g in range(units // 2):
        slot = g % 2
        for t in range(STACK):
            for c2 in range(2):
                u = 2 * g + c2
                some = pl.ds(t * KEEP * deep + u // STACK, KEEP, stride=deep)
                for q in range(shards // fold):
                    cols = pl.ds(q * LANES, LANES)
                    value = vals[u % STACK, q, some, :]
                    where = freqs[u % STACK, q, some, :]
                    power = jnp.sum(value * value, axis=0, keepdims=True)
                    value = value * (lax.rsqrt(power / GROUP + 1e-06) * (-STEP))
                    s = jnp.zeros((GROUP, LANES), F32)
                    for j in range(KEEP):
                        s = jnp.where(freq == where[j : j + 1], value[j : j + 1], s)
                    spec[slot, pl.ds((2 * t + c2) * GROUP, GROUP), cols] = s.astype(BF16)
        y = lax.dot_general(tokens[:, pl.ds(g * depth, depth)], spec[slot], NN, preferred_element_type=F32)
        out[...] = y if g == 0 else out[...] + y


def old_kernel(shard_rows, mine, theirs, weight, change, own, other):
    nz, pair, width = weight.shape
    batch = mine.shape[0]
    step = 512
    x = [mine, theirs]
    y = [own, other]
    for p in range(2):
        acc = change[p * batch : (p + 1) * batch, :]
        for k in range(width // step):
            cols = pl.ds(k * step, step)
            w = jnp.concatenate(
                [weight[z, h * shard_rows : (h + 1) * shard_rows, cols] for h in range(pair // shard_rows) for z in range(nz)],
                axis=0,
            )
            part = lax.dot_general(x[p][:, cols], w, NT, preferred_element_type=F32)
            acc = acc + part * (1.0 - STEP * DECAY)
        y[p][...] = acc


def swap(x, axis):
    return lax.ppermute(x, axis, [(0, 1), (1, 0)])


def body(sizes, tokens, momentum, gradient, weight, kept_index):
    nx, nyl, nc, nyh, nz = sizes
    rows, width = weight.shape
    half = width // nc
    groups = width // (STACK * LANES)
    units = groups
    deep = -(-units // STACK)
    shards = nyh * nz
    batch = tokens.shape[0]
    pair = basis_pair()
    high = pair.astype(jnp.bfloat16)
    low = (pair - high.astype(np.float32)).astype(jnp.bfloat16)
    core = lax.axis_index("core")

    own = lax.dynamic_slice(weight, (0, core * half), (rows, half))
    far = swap(own, "yhi")
    first = lax.axis_index("yhi") == 0
    duo = jnp.concatenate([jnp.where(first, own, far), jnp.where(first, far, own)], axis=0)
    old_all = lax.all_gather(duo, "z", axis=0, tiled=False)

    mine = lax.dynamic_slice(tokens, (0, core * half), (batch, half))
    theirs = swap(lax.dynamic_slice(tokens, (0, (1 - core) * half), (batch, half)), "core")

    order = kept_index.reshape(rows, groups, STACK, 2, KEEP).transpose(4, 1, 3, 2, 0)
    lines = STACK * KEEP * deep
    kept, idx_all, new_momentum = call(
        functools.partial(local_kernel, nc),
        (
            jax.ShapeDtypeStruct((nc * lines, LANES), F32),
            jax.ShapeDtypeStruct((nc * lines, LANES), F32),
            jax.ShapeDtypeStruct((rows, width), F32),
        ),
        (momentum[0], gradient[0], order.reshape(KEEP * nc * units, LANES), jnp.asarray(pair)),
        flops=24 * rows * width * LANES,
        scratch_shapes=[pltpu.VMEM((STACK, deep, nc * KEEP, LANES), F32)] * 2,
    )
    idx_own = lax.dynamic_index_in_dim(idx_all.reshape(STACK, nc, KEEP * deep, LANES), core, 1, keepdims=False)
    idx_own = idx_own.reshape(lines, LANES)

    pieces = lax.all_to_all(kept.reshape(nyl * nc * nx, 1, deep * LANES), ("ylo", "core", "x"), 0, 0, tiled=True)
    total = to_all(jnp.sum(pieces, axis=0), ("ylo", "x"), nyl * nx).reshape(lines, LANES)
    both = to_all(jnp.concatenate([total.astype(BF16), idx_own.astype(BF16)], axis=0), ("yhi", "z"), shards)

    wide = pltpu.VMEM((STACK, KEEP * deep, LANES), F32)
    own_new = call(
        weight_kernel,
        jax.ShapeDtypeStruct((rows, half), BF16),
        (total, idx_own, jnp.asarray(pair), own),
        flops=12 * rows * half * LANES,
        scratch_shapes=[wide, wide],
    )
    other_new = swap(own_new, "core")
    left = core == 0
    new_weight = jnp.concatenate([jnp.where(left, own_new, other_new), jnp.where(left, other_new, own_new)], axis=1)

    turned = call(
        tokens_kernel,
        jax.ShapeDtypeStruct((nc * batch, half), BF16),
        (mine, theirs, jnp.asarray(high), jnp.asarray(low)),
        flops=4 * nc * batch * half * LANES,
    )
    change = call(
        functools.partial(direction_kernel, rows, units),
        jax.ShapeDtypeStruct((nc * batch, shards * rows), F32),
        (both, turned),
        flops=4 * nc * batch * half * shards * rows,
        scratch_shapes=[
            pltpu.VMEM((STACK, shards * rows // LANES, lines, LANES), F32),
            pltpu.VMEM((STACK, shards * rows // LANES, lines, LANES), jnp.int32),
            pltpu.VMEM((2, 2 * STACK * GROUP, shards * rows), BF16),
        ],
    )
    part = jax.ShapeDtypeStruct((batch, shards * rows), F32)
    here, there = call(
        functools.partial(old_kernel, rows),
        (part, part),
        (mine, theirs, old_all, change),
        flops=2 * nc * batch * half * shards * rows,
    )
    projected = (here + swap(there, "core")).astype(BF16)
    return new_weight, new_momentum[None], projected


def run(sizes, devices):
    fine = Mesh(devices.reshape(sizes), AXES)
    rep, fsdp = AXES[:3], AXES[3:]
    return jax.shard_map(
        functools.partial(body, sizes),
        mesh=fine,
        in_specs=(P(AXES, None), P(rep, fsdp, None), P(rep, fsdp, None), P(fsdp, None), P(fsdp, None, None)),
        out_specs=(P(fsdp, None), P(rep, fsdp, None), P(AXES, None)),
        check_vma=False,
    )


def solution(mesh):
    return run((8, 4, 2, 2, 8), mesh.devices)
```

```python
import functools
import math

import jax
import jax.numpy as jnp
import numpy as np
from jax import lax
from jax.experimental import pallas as pl
from jax.experimental.pallas import tpu as pltpu
from jax.sharding import Mesh
from jax.sharding import PartitionSpec as P

GROUP = 64
KEEP = 8
LANES = 128
STACK = 4
HIGHEST = lax.Precision.HIGHEST
STEP = 0.01
DECAY = 0.1
AXES = ("x", "ylo", "core", "yhi", "z")
F32 = jnp.float32
BF16 = jnp.bfloat16
NT = (((1,), (1,)), ((), ()))
NN = (((1,), (0,)), ((), ()))
TN = (((0,), (0,)), ((), ()))


def basis_pair():
    k = np.arange(GROUP)[:, None]
    n = np.arange(GROUP)[None, :]
    scale = np.where(k == 0, math.sqrt(1.0 / GROUP), math.sqrt(2.0 / GROUP))
    table = scale * np.cos(np.pi * (n + 0.5) * k / GROUP)
    return np.kron(np.eye(2), table).astype(np.float32)


def call(kernel, out_shape, args, flops, vmem=12, **kw):
    size = sum(a.size * a.dtype.itemsize for a in args)
    return pl.pallas_call(
        kernel,
        out_shape=out_shape,
        compiler_params=pltpu.CompilerParams(vmem_limit_bytes=vmem * 1024 * 1024),
        cost_estimate=pl.CostEstimate(flops=flops, bytes_accessed=size, transcendentals=0),
        **kw,
    )(*args)


def to_all(x, axes, parts):
    copies = lax.optimization_barrier(jnp.broadcast_to(x[None], (parts,) + x.shape))
    return lax.all_to_all(copies, axes, 0, 0, tiled=True)


def pick(sources, rows):
    lane = lax.broadcasted_iota(jnp.int32, sources[0][0].shape, 1) // rows
    merged = None
    for s, (block, group) in enumerate(sources):
        moved = block
        if group != s:
            moved = pltpu.roll(block, ((s - group) % len(sources)) * rows, axis=1)
        merged = moved if merged is None else jnp.where(lane == s, moved, merged)
    return merged


def regroup(blocks, rows, target):
    return pick([(block, target) for block in blocks], rows)


def split(x, axis, order):
    high = x.astype(BF16)
    low = (x - high.astype(F32)).astype(BF16)
    return jnp.concatenate([high, low, high] if order else [high, high, low], axis=axis)


def index_kernel(units, core, idx, out):
    total_units = idx.shape[0] // KEEP
    rows = LANES // STACK
    block = [idx[pl.ds(core[0] * units + u, KEEP, stride=total_units), :].astype(F32) for u in range(units)]
    full = units // STACK
    parts = []
    for r in range(full):
        for t in range(STACK):
            parts.append(regroup(block[r * STACK : (r + 1) * STACK], rows, t))
    if full * STACK < units:
        for t in range(0, STACK, 2):
            parts.append(pick([(block[full * STACK + s % 2], t + s // 2) for s in range(STACK)], rows))
    out[...] = jnp.concatenate(parts, axis=0).astype(BF16)


def join_kernel(own, far, own_idx, far_idx, out):
    rows, width = own.shape
    tiles = width // LANES
    size = out.shape[0] // 2
    for h, (weight, idx) in enumerate(((own, own_idx), (far, far_idx))):
        for c in range(tiles):
            out[h * size + c * rows : h * size + (c + 1) * rows, :] = weight[:, c * LANES : (c + 1) * LANES]
        out[h * size + tiles * rows : (h + 1) * size, :] = idx[...]


def local_kernel(cores, mom, grad, idx, b2, kept, new_mom, kept_wide):
    rows = mom.shape[0]
    total_units = idx.shape[0] // KEEP
    units = total_units // cores
    deep = kept_wide.shape[1]
    forward = split(b2[...], 1, False)
    back = split(b2[...], 0, False)
    freq = lax.broadcasted_iota(jnp.int32, (GROUP, LANES), 0)
    kept_wide[...] = jnp.zeros_like(kept_wide)
    for g in range(total_units // 2):
        tiles = []
        for t in range(STACK):
            cols = pl.ds((STACK * g + t) * LANES, LANES)
            tiles.append(0.9 * mom[:, cols] + grad[:, cols].astype(F32))
        block = jnp.concatenate(tiles, axis=0)
        spec = lax.dot_general(forward, split(block, 1, True), NT, preferred_element_type=F32)
        parts = []
        for c2 in range(2):
            whole = 2 * g + c2
            core, u = whole // units, whole % units
            half = spec[c2 * GROUP : (c2 + 1) * GROUP]
            sent = jnp.zeros_like(half)
            for j in range(KEEP):
                line = j * total_units + whole
                one = jnp.where(freq == idx[line : line + 1, :], half, 0.0)
                at = core * KEEP + j
                kept_wide[u % STACK, u // STACK, at : at + 1, :] = jnp.sum(one, axis=0, keepdims=True)
                sent = sent + one
            parts.append(sent)
        sent = lax.dot_general(split(jnp.concatenate(parts, axis=0), 0, True), back, TN, preferred_element_type=F32)
        rest = block - sent
        for t in range(STACK):
            new_mom[:, pl.ds((STACK * g + t) * LANES, LANES)] = rest[t * rows : (t + 1) * rows]
    both = cores * KEEP
    for ur in range(deep):
        for t in range(STACK):
            lines = pl.ds(t * both * deep + ur, both, stride=deep)
            kept[lines, :] = regroup([kept_wide[b, ur] for b in range(STACK)], rows, t)


def weight_kernel(core, tot, idx, b2, old, new, tot_wide):
    rows, width = old.shape
    deep = tot.shape[0] // (STACK * KEEP)
    span = KEEP * deep
    total_units = idx.shape[0] // KEEP
    units = 2 * width // (STACK * LANES)
    for b in range(STACK):
        tot_wide[b] = regroup([tot[t * span : (t + 1) * span, :] for t in range(STACK)], rows, b)
    freq = lax.broadcasted_iota(jnp.int32, (GROUP, LANES), 0)
    for g in range(units // 2):
        parts = []
        for c2 in range(2):
            u = 2 * g + c2
            value = tot_wide[u % STACK, pl.ds(u // STACK, KEEP, stride=deep), :]
            where = idx[pl.ds(core[0] * units + u, KEEP, stride=total_units), :]
            power = jnp.sum(value * value, axis=0, keepdims=True)
            value = value * lax.rsqrt(power / GROUP + 1e-06)
            spec = jnp.zeros((GROUP, LANES), F32)
            for j in range(KEEP):
                spec = jnp.where(freq == where[j : j + 1], value[j : j + 1], spec)
            parts.append(spec)
        direction = lax.dot_general(
            jnp.concatenate(parts, axis=0), b2[...], TN, precision=HIGHEST, preferred_element_type=F32
        )
        for t in range(STACK):
            cols = pl.ds((STACK * g + t) * LANES, LANES)
            kept_part = old[:, cols].astype(F32) * (1.0 - STEP * DECAY)
            new[:, cols] = (kept_part - STEP * direction[t * rows : (t + 1) * rows]).astype(BF16)


def tokens_kernel(mine, theirs, high, low, out):
    batch = mine.shape[0]
    for t in range(mine.shape[1] // LANES):
        cols = pl.ds(t * LANES, LANES)
        x = jnp.concatenate([mine[:, cols], theirs[:, cols]], axis=0)
        y = lax.dot_general(x, high[...], NT, preferred_element_type=F32)
        y = y + lax.dot_general(x, low[...], NT, preferred_element_type=F32)
        out[:, cols] = y.astype(BF16)


def pack_kernel(units, tot, out):
    deep = tot.shape[0] // (STACK * KEEP)
    full = units // STACK
    lane = lax.broadcasted_iota(jnp.int32, (KEEP, LANES), 1)
    blocks = [[tot[pl.ds(t * KEEP * deep + r, KEEP, stride=deep), :] for t in range(STACK)] for r in range(deep)]
    parts = []
    for r in range(full):
        parts += blocks[r]
    if full < deep:
        for t in range(0, STACK, 2):
            upper = pltpu.roll(blocks[full][t + 1], LANES // 2, axis=1)
            parts.append(jnp.where(lane < LANES // 2, blocks[full][t], upper))
    packed = jnp.concatenate(parts, axis=0).astype(BF16)
    for f in range(out.shape[0]):
        out[f] = packed


def product_kernel(rows, units, place, sums, tokens, mine, theirs, source, own, other, weight, vals, freqs, spec, sems):
    shards, lines, _ = sums.shape
    nz, size, _ = source.shape
    size = size // 2
    steps = units // 2
    high = STACK * rows
    fold = LANES // rows
    full = units // STACK

    def copy(h, k):
        at = h * size + (steps * high if k == steps else k * high)
        part = pl.ds(at, lines if k == steps else high)
        return pltpu.make_async_copy(source.at[:, part, :], weight.at[:, part, :], sems.at[h, k])

    for k in [steps] + list(range(steps)):
        for h in range(2):
            copy(h, k).start()

    def start_of(y):
        h = place[0] if y == 0 else 1 - place[0]
        return h * size

    def spread(blocks, out, q):
        for b in range(STACK):
            out[b, q] = regroup(blocks, rows, b)

    for q in range(shards // fold):
        spread([sums[fold * q + f].astype(F32) for f in range(fold)], vals, q)
    for h in range(2):
        copy(h, steps).wait()
    for q in range(shards // fold):
        blocks = []
        for f in range(fold * q, fold * (q + 1)):
            at = pl.multiple_of(start_of(f // nz) + steps * high, 16)
            blocks.append(weight[f % nz, pl.ds(at, lines), :].astype(F32))
        spread(blocks, freqs, q)
    pack = 16
    freq = lax.broadcasted_iota(jnp.int32, (GROUP, LANES), 0).astype(F32).astype(BF16)
    freq = [freq[k * pack : (k + 1) * pack] for k in range(GROUP // pack)]
    depth = 2 * STACK * GROUP
    batch = mine.shape[0]
    wide = nz * rows
    for g in range(steps):
        slot = g % 2
        for t in range(STACK):
            for c2 in range(2):
                u = 2 * g + c2
                if u // STACK < full:
                    lane, line = u % STACK, (u // STACK * STACK + t) * KEEP
                else:
                    lane, line = 2 * (t % 2) + u % STACK, (full * STACK + t // 2) * KEEP
                for q in range(shards // fold):
                    cols = pl.ds(q * LANES, LANES)
                    value = vals[lane, q, line : line + KEEP, :]
                    where = freqs[lane, q, line : line + KEEP, :]
                    power = jnp.sum(value * value, axis=0, keepdims=True)
                    value = value * (lax.rsqrt(power / GROUP + 1e-06) * (-STEP))
                    s = [jnp.zeros((pack, LANES), BF16)] * len(freq)
                    for j in range(KEEP):
                        v = jnp.broadcast_to(value[j : j + 1], (pack, LANES)).astype(BF16)
                        w = jnp.broadcast_to(where[j : j + 1], (pack, LANES)).astype(BF16)
                        s = [jnp.where(f == w, v, old) for f, old in zip(freq, s)]
                    spec[slot, pl.ds((2 * t + c2) * GROUP, GROUP), cols] = jnp.concatenate(s, axis=0)
        for h in range(2):
            copy(h, g).wait()
        cols = pl.ds(g * depth, depth)
        for y in range(2):
            at = start_of(y) + g * high
            tiles = []
            for c in range(STACK):
                line = pl.multiple_of(at + c * rows, 16)
                tiles.append(jnp.concatenate([weight[z, pl.ds(line, rows), :] for z in range(nz)], axis=0))
            w = jnp.concatenate(tiles, axis=1)
            lanes = pl.ds(y * wide, wide)
            for p, (x, out) in enumerate(((mine, own), (theirs, other))):
                part = lax.dot_general(x[:, cols], w, NT, preferred_element_type=F32) * (1.0 - STEP * DECAY)
                part += lax.dot_general(
                    tokens[p * batch : (p + 1) * batch, cols], spec[slot, :, lanes], NN, preferred_element_type=F32
                )
                out[:, lanes] = part if g == 0 else out[:, lanes] + part


def swap(x, axis):
    return lax.ppermute(x, axis, [(0, 1), (1, 0)])


def body(sizes, tokens, momentum, gradient, weight, kept_index):
    nx, nyl, nc, nyh, nz = sizes
    rows, width = weight.shape
    half = width // nc
    groups = width // (STACK * LANES)
    units = groups
    deep = -(-units // STACK)
    shards = nyh * nz
    batch = tokens.shape[0]
    pair = basis_pair()
    high = pair.astype(jnp.bfloat16)
    low = (pair - high.astype(np.float32)).astype(jnp.bfloat16)
    core = lax.axis_index("core")

    own = lax.dynamic_slice(weight, (0, core * half), (rows, half))
    far = swap(own, "yhi")
    order = kept_index.reshape(rows, groups, STACK, 2, KEEP).transpose(4, 1, 3, 2, 0).reshape(KEEP * nc * units, LANES)
    smem = pl.BlockSpec(memory_space=pltpu.SMEM)
    vmem = pl.BlockSpec(memory_space=pltpu.VMEM)
    core_ref = core.reshape(1)
    idx_own = call(
        functools.partial(index_kernel, units),
        jax.ShapeDtypeStruct((KEEP * units, LANES), BF16),
        (core_ref, order),
        flops=1000,
        in_specs=[smem, vmem],
    )
    idx_far = swap(idx_own, "yhi")
    lines = STACK * KEEP * deep
    kept, new_momentum = call(
        functools.partial(local_kernel, nc),
        (
            jax.ShapeDtypeStruct((nc * lines, LANES), F32),
            jax.ShapeDtypeStruct((rows, width), F32),
        ),
        (momentum[0], gradient[0], order, jnp.asarray(pair)),
        flops=12 * rows * width * LANES,
        scratch_shapes=[pltpu.VMEM((STACK, deep, nc * KEEP, LANES), F32)],
    )
    far, idx_far, kept = lax.optimization_barrier((far, idx_far, kept))
    size = half // LANES * rows + KEEP * units
    duo = call(
        join_kernel,
        jax.ShapeDtypeStruct((2 * size, LANES), BF16),
        (own, far, idx_own, idx_far),
        flops=1000,
    )
    duo, kept = lax.optimization_barrier((duo, kept))
    old_all = lax.all_gather(duo, "z", axis=0, tiled=False)

    pieces = lax.all_to_all(kept.reshape(nyl * nc * nx, 1, deep * LANES), ("ylo", "core", "x"), 0, 0, tiled=True)
    total = to_all(jnp.sum(pieces, axis=0), ("ylo", "x"), nyl * nx).reshape(lines, LANES)
    copies = call(
        functools.partial(pack_kernel, units),
        jax.ShapeDtypeStruct((shards, KEEP * units, LANES), BF16),
        (total,),
        flops=1000,
    )
    sums = lax.all_to_all(copies, ("yhi", "z"), 0, 0, tiled=True)

    mine = lax.dynamic_slice(tokens, (0, core * half), (batch, half))
    theirs = swap(lax.dynamic_slice(tokens, (0, (1 - core) * half), (batch, half)), "core")

    own_new = call(
        weight_kernel,
        jax.ShapeDtypeStruct((rows, half), BF16),
        (core_ref, total, order, jnp.asarray(pair), own),
        flops=12 * rows * half * LANES,
        in_specs=[smem, vmem, vmem, vmem, vmem],
        scratch_shapes=[pltpu.VMEM((STACK, KEEP * deep, LANES), F32)],
    )
    other_new = swap(own_new, "core")
    left = core == 0
    new_weight = jnp.concatenate([jnp.where(left, own_new, other_new), jnp.where(left, other_new, own_new)], axis=1)

    turned = call(
        tokens_kernel,
        jax.ShapeDtypeStruct((nc * batch, half), BF16),
        (mine, theirs, jnp.asarray(high), jnp.asarray(low)),
        flops=4 * nc * batch * half * LANES,
    )
    out_width = shards * rows
    part = jax.ShapeDtypeStruct((batch, out_width), F32)
    table = pltpu.VMEM((STACK, out_width // LANES, KEEP * units, LANES), F32)
    here, there = call(
        functools.partial(product_kernel, rows, units),
        (part, part),
        (lax.axis_index("yhi").reshape(1), sums, turned, mine, theirs, old_all),
        flops=6 * nc * batch * half * out_width,
        vmem=20,
        in_specs=[smem, vmem, vmem, vmem, vmem, pl.BlockSpec(memory_space=pl.ANY)],
        scratch_shapes=[
            pltpu.VMEM((nz, 2 * size, LANES), BF16),
            table,
            table,
            pltpu.VMEM((2, 2 * STACK * GROUP, out_width), BF16),
            pltpu.SemaphoreType.DMA((2, units // 2 + 1)),
        ],
    )
    projected = (here + swap(there, "core")).astype(BF16)
    return new_weight, new_momentum[None], projected


def run(sizes, devices):
    fine = Mesh(devices.reshape(sizes), AXES)
    rep, fsdp = AXES[:3], AXES[3:]
    return jax.shard_map(
        functools.partial(body, sizes),
        mesh=fine,
        in_specs=(P(AXES, None), P(rep, fsdp, None), P(rep, fsdp, None), P(fsdp, None), P(fsdp, None, None)),
        out_specs=(P(fsdp, None), P(rep, fsdp, None), P(AXES, None)),
        check_vma=False,
    )


def solution(mesh):
    return run((8, 4, 2, 2, 8), mesh.devices)
```

```python
import functools
import math

import jax
import jax.numpy as jnp
import numpy as np
from jax import lax
from jax.experimental import pallas as pl
from jax.experimental.pallas import tpu as pltpu
from jax.sharding import Mesh
from jax.sharding import PartitionSpec as P

GROUP = 64
KEEP = 8
LANES = 128
STACK = 4
HIGHEST = lax.Precision.HIGHEST
STEP = 0.01
DECAY = 0.1
AXES = ("x", "ylo", "core", "yhi", "z")
F32 = jnp.float32
BF16 = jnp.bfloat16
NT = (((1,), (1,)), ((), ()))
NN = (((1,), (0,)), ((), ()))
TN = (((0,), (0,)), ((), ()))


def basis_pair():
    k = np.arange(GROUP)[:, None]
    n = np.arange(GROUP)[None, :]
    scale = np.where(k == 0, math.sqrt(1.0 / GROUP), math.sqrt(2.0 / GROUP))
    table = scale * np.cos(np.pi * (n + 0.5) * k / GROUP)
    return np.kron(np.eye(2), table).astype(np.float32)


def call(kernel, out_shape, args, flops, vmem=12, **kw):
    return pl.pallas_call(
        kernel,
        out_shape=out_shape,
        compiler_params=pltpu.CompilerParams(vmem_limit_bytes=vmem * 1024 * 1024),
        cost_estimate=pl.CostEstimate(flops=flops, bytes_accessed=0, transcendentals=0),
        **kw,
    )(*args)


def to_all(x, axes, parts):
    copies = lax.optimization_barrier(jnp.broadcast_to(x[None], (parts,) + x.shape))
    return lax.all_to_all(copies, axes, 0, 0, tiled=True)


def pick(sources, rows):
    lane = lax.broadcasted_iota(jnp.int32, sources[0][0].shape, 1) // rows
    merged = None
    for s, (block, group) in enumerate(sources):
        moved = block
        if group != s:
            moved = pltpu.roll(block, ((s - group) % len(sources)) * rows, axis=1)
        merged = moved if merged is None else jnp.where(lane == s, moved, merged)
    return merged


def regroup(blocks, rows, target):
    return pick([(block, target) for block in blocks], rows)


def split(x, axis, order):
    high = x.astype(BF16)
    low = (x - high.astype(F32)).astype(BF16)
    return jnp.concatenate([high, low, high] if order else [high, high, low], axis=axis)


def join_kernel(units, core, weight, idx, out):
    rows, width = weight.shape
    tiles = width // 2 // LANES
    for c in range(tiles):
        at = pl.multiple_of(core[0] * (width // 2) + c * LANES, LANES)
        out[c * rows : (c + 1) * rows, :] = weight[:, pl.ds(at, LANES)]
    total_units = idx.shape[0] // KEEP
    block = [idx[pl.ds(core[0] * units + u, KEEP, stride=total_units), :].astype(F32) for u in range(units)]
    full = units // STACK
    parts = []
    for r in range(full):
        for t in range(STACK):
            parts.append(regroup(block[r * STACK : (r + 1) * STACK], rows, t))
    if full * STACK < units:
        for t in range(0, STACK, 2):
            parts.append(pick([(block[full * STACK + s % 2], t + s // 2) for s in range(STACK)], rows))
    out[tiles * rows :, :] = jnp.concatenate(parts, axis=0).astype(BF16)


def local_kernel(cores, mom, grad, idx, b2, kept, new_mom, kept_wide):
    rows = mom.shape[0]
    total_units = idx.shape[0] // KEEP
    units = total_units // cores
    deep = kept_wide.shape[1]
    forward = split(b2[...], 1, False)
    back = split(b2[...], 0, False)
    freq = lax.broadcasted_iota(jnp.int32, (GROUP, LANES), 0)
    kept_wide[...] = jnp.zeros_like(kept_wide)
    for g in range(total_units // 2):
        tiles = []
        for t in range(STACK):
            cols = pl.ds((STACK * g + t) * LANES, LANES)
            tiles.append(0.9 * mom[:, cols] + grad[:, cols].astype(F32))
        block = jnp.concatenate(tiles, axis=0)
        spec = lax.dot_general(forward, split(block, 1, True), NT, preferred_element_type=F32)
        parts = []
        for c2 in range(2):
            whole = 2 * g + c2
            core, u = whole // units, whole % units
            half = spec[c2 * GROUP : (c2 + 1) * GROUP]
            sent = jnp.zeros_like(half)
            for j in range(KEEP):
                line = j * total_units + whole
                one = jnp.where(freq == idx[line : line + 1, :], half, 0.0)
                at = core * KEEP + j
                kept_wide[u % STACK, u // STACK, at : at + 1, :] = jnp.sum(one, axis=0, keepdims=True)
                sent = sent + one
            parts.append(sent)
        sent = lax.dot_general(split(jnp.concatenate(parts, axis=0), 0, True), back, TN, preferred_element_type=F32)
        rest = block - sent
        for t in range(STACK):
            new_mom[:, pl.ds((STACK * g + t) * LANES, LANES)] = rest[t * rows : (t + 1) * rows]
    both = cores * KEEP
    for ur in range(deep):
        for t in range(STACK):
            lines = pl.ds(t * both * deep + ur, both, stride=deep)
            kept[lines, :] = regroup([kept_wide[b, ur] for b in range(STACK)], rows, t)


def tokens_kernel(mine, theirs, high, low, out):
    batch = mine.shape[0]
    for t in range(mine.shape[1] // LANES):
        cols = pl.ds(t * LANES, LANES)
        x = jnp.concatenate([mine[:, cols], theirs[:, cols]], axis=0)
        y = lax.dot_general(x, high[...], NT, preferred_element_type=F32)
        y = y + lax.dot_general(x, low[...], NT, preferred_element_type=F32)
        out[:, cols] = y.astype(BF16)


def pack_kernel(units, rows, tot, out, flat):
    fold = LANES // rows
    shards = out.shape[1] // units * fold
    deep = tot.shape[0] // shards
    nq = shards // fold
    for r in range(deep):
        blocks = [tot[pl.ds(f * deep + r, nq, stride=fold * deep), :] for f in range(fold)]
        for b in range(min(STACK, units - r * STACK)):
            u = r * STACK + b
            flat[u * nq : (u + 1) * nq, :] = regroup(blocks, rows, b)
    packed = flat[...].astype(BF16)
    for c in range(out.shape[0]):
        out[c] = packed


def product_kernel(
    rows, units, place, sums, tokens, mine, theirs, idx, b2, old, source, own, other, new, weight, vals, freqs, spec, sems
):
    nz, size, _ = source.shape
    size = size // 2
    shards = 2 * nz
    nq = shards * rows // LANES
    lines = KEEP * units
    stride = units * nq
    steps = units // 2
    high = STACK * rows
    fold = LANES // rows
    full = units // STACK

    def copy(h, k):
        at = h * size + (steps * high if k == steps else k * high)
        part = pl.ds(at, lines if k == steps else high)
        return pltpu.make_async_copy(source.at[:, part, :], weight.at[:, part, :], sems.at[h, k])

    for k in [steps] + list(range(steps)):
        for h in range(2):
            copy(h, k).start()

    def start_of(y):
        h = place[0] if y == 0 else 1 - place[0]
        return h * size

    def spread(blocks, out, q):
        for b in range(STACK):
            out[b, q] = regroup(blocks, rows, b)

    for k in range(STACK * KEEP):
        vals[k * stride : (k + 1) * stride, :] = sums[k].astype(F32)

    def coefficients(t, u, q):
        value = vals[pl.ds(t * KEEP * stride + u * nq + q, KEEP, stride=stride), :]
        power = jnp.sum(value * value, axis=0, keepdims=True)
        return value * (lax.rsqrt(power / GROUP + 1e-06) * (-STEP))

    shard = place[0] * nz + place[1]
    lane = lax.broadcasted_iota(jnp.int32, (KEEP, LANES), 1) // rows
    line = lax.broadcasted_iota(jnp.int32, (GROUP, LANES), 0)
    total_units = idx.shape[0] // KEEP
    batch = mine.shape[0]
    for g in range(steps):
        parts = []
        for c2 in range(2):
            u = 2 * g + c2
            value = None
            for t in range(STACK):
                moved = pltpu.roll(coefficients(t, u, shard // fold), lax.rem(t - shard % fold + fold, fold) * rows, axis=1)
                value = moved if value is None else jnp.where(lane == t, moved, value)
            where = idx[pl.ds(place[2] * units + u, KEEP, stride=total_units), :]
            s = jnp.zeros((GROUP, LANES), F32)
            for j in range(KEEP):
                s = jnp.where(line == where[j : j + 1], value[j : j + 1], s)
            parts.append(s)
        change = lax.dot_general(
            split(jnp.concatenate(parts, axis=0), 0, True), b2[...], TN, preferred_element_type=F32
        )
        for t in range(STACK):
            at = pl.multiple_of(place[2] * (old.shape[1] // 2) + (STACK * g + t) * LANES, LANES)
            fresh = old[:, pl.ds(at, LANES)].astype(F32) * (1.0 - STEP * DECAY) + change[t * rows : (t + 1) * rows]
            fresh = fresh.astype(BF16)
            new[:, (STACK * g + t) * LANES : (STACK * g + t + 1) * LANES] = fresh
            other[batch + g * rows : batch + (g + 1) * rows, t * LANES : (t + 1) * LANES] = fresh.astype(F32)

    for h in range(2):
        copy(h, steps).wait()
    for q in range(shards // fold):
        blocks = []
        for f in range(fold * q, fold * (q + 1)):
            at = pl.multiple_of(start_of(f // nz) + steps * high, 16)
            blocks.append(weight[f % nz, pl.ds(at, lines), :].astype(F32))
        spread(blocks, freqs, q)
    pack = 16
    freq = lax.broadcasted_iota(jnp.int32, (GROUP, LANES), 0).astype(F32).astype(BF16)
    freq = [freq[k * pack : (k + 1) * pack] for k in range(GROUP // pack)]
    depth = 2 * STACK * GROUP
    wide = nz * rows
    for g in range(steps):
        slot = g % 2
        for t in range(STACK):
            for c2 in range(2):
                u = 2 * g + c2
                if u // STACK < full:
                    lane, line = u % STACK, (u // STACK * STACK + t) * KEEP
                else:
                    lane, line = 2 * (t % 2) + u % STACK, (full * STACK + t // 2) * KEEP
                for q in range(shards // fold):
                    cols = pl.ds(q * LANES, LANES)
                    value = coefficients(t, u, q)
                    where = freqs[lane, q, line : line + KEEP, :]
                    s = [jnp.zeros((pack, LANES), BF16)] * len(freq)
                    for j in range(KEEP):
                        v = jnp.broadcast_to(value[j : j + 1], (pack, LANES)).astype(BF16)
                        w = jnp.broadcast_to(where[j : j + 1], (pack, LANES)).astype(BF16)
                        s = [jnp.where(f == w, v, old) for f, old in zip(freq, s)]
                    spec[slot, pl.ds((2 * t + c2) * GROUP, GROUP), cols] = jnp.concatenate(s, axis=0)
        for h in range(2):
            copy(h, g).wait()
        cols = pl.ds(g * depth, depth)
        for y in range(2):
            at = start_of(y) + g * high
            tiles = []
            for c in range(STACK):
                line = pl.multiple_of(at + c * rows, 16)
                tiles.append(jnp.concatenate([weight[z, pl.ds(line, rows), :] for z in range(nz)], axis=0))
            w = jnp.concatenate(tiles, axis=1)
            lanes = pl.ds(y * wide, wide)
            for p, (x, out) in enumerate(((mine, own), (theirs, other))):
                part = lax.dot_general(x[:, cols], w, NT, preferred_element_type=F32) * (1.0 - STEP * DECAY)
                part += lax.dot_general(
                    tokens[p * batch : (p + 1) * batch, cols], spec[slot, :, lanes], NN, preferred_element_type=F32
                )
                out[:batch, lanes] = part if g == 0 else out[:batch, lanes] + part


def finish_kernel(core, own, received, new, projected, new_weight):
    batch = own.shape[0]
    rows, half = new.shape
    projected[...] = (own[...] + received[:batch, : own.shape[1]]).astype(BF16)
    new_weight[:, pl.ds(pl.multiple_of(core[0] * half, LANES), half)] = new[...]
    for c in range(half // LANES):
        t, g = c % STACK, c // STACK
        at = pl.multiple_of((1 - core[0]) * half + c * LANES, LANES)
        block = received[batch + g * rows : batch + (g + 1) * rows, t * LANES : (t + 1) * LANES]
        new_weight[:, pl.ds(at, LANES)] = block.astype(BF16)


def swap(x, axis):
    return lax.ppermute(x, axis, [(0, 1), (1, 0)])


def body(sizes, tokens, momentum, gradient, weight, kept_index):
    nx, nyl, nc, nyh, nz = sizes
    rows, width = weight.shape
    half = width // nc
    groups = width // (STACK * LANES)
    units = groups
    deep = -(-units // STACK)
    shards = nyh * nz
    batch = tokens.shape[0]
    pair = basis_pair()
    high = pair.astype(jnp.bfloat16)
    low = (pair - high.astype(np.float32)).astype(jnp.bfloat16)
    core = lax.axis_index("core")

    order = kept_index.reshape(rows, groups, STACK, 2, KEEP).transpose(4, 1, 3, 2, 0).reshape(KEEP * nc * units, LANES)
    smem = pl.BlockSpec(memory_space=pltpu.SMEM)
    vmem = pl.BlockSpec(memory_space=pltpu.VMEM)
    core_ref = core.reshape(1)
    size = half // LANES * rows + KEEP * units
    near = call(
        functools.partial(join_kernel, units),
        jax.ShapeDtypeStruct((size, LANES), BF16),
        (core_ref, weight, order),
        flops=0,
        in_specs=[smem, vmem, vmem],
    )
    far = swap(near, "yhi")
    kept, new_momentum = call(
        functools.partial(local_kernel, nc),
        (
            jax.ShapeDtypeStruct((nc * STACK * KEEP * deep, LANES), F32),
            jax.ShapeDtypeStruct((rows, width), F32),
        ),
        (momentum[0], gradient[0], order, jnp.asarray(pair)),
        flops=0,
        scratch_shapes=[pltpu.VMEM((STACK, deep, nc * KEEP, LANES), F32)],
    )
    far, kept = lax.optimization_barrier((far, kept))
    duo, kept = lax.optimization_barrier((jnp.concatenate([near, far], axis=0), kept))
    old_all = lax.all_gather(duo, "z", axis=0, tiled=False)

    pieces = lax.all_to_all(kept.reshape(nyl * nc * nx, 1, deep * LANES), ("ylo", "core", "x"), 0, 0, tiled=True)
    total = to_all(jnp.sum(pieces, axis=0), ("yhi", "z"), shards).reshape(shards * deep, LANES)
    stride = units * shards * rows // LANES
    copies = call(
        functools.partial(pack_kernel, units, rows),
        jax.ShapeDtypeStruct((nyl * nx, stride, LANES), BF16),
        (total,),
        flops=0,
        scratch_shapes=[pltpu.VMEM((stride, LANES), F32)],
    )
    sums = lax.all_to_all(copies, ("ylo", "x"), 0, 0, tiled=True)

    mine = lax.dynamic_slice(tokens, (0, core * half), (batch, half))
    theirs = swap(lax.dynamic_slice(tokens, (0, (1 - core) * half), (batch, half)), "core")
    turned = call(
        tokens_kernel,
        jax.ShapeDtypeStruct((nc * batch, half), BF16),
        (mine, theirs, jnp.asarray(high), jnp.asarray(low)),
        flops=0,
    )
    out_width = shards * rows
    back = jnp.asarray(np.concatenate([high, high, low], axis=0))
    here, there, own_new = call(
        functools.partial(product_kernel, rows, units),
        (
            jax.ShapeDtypeStruct((batch, out_width), F32),
            jax.ShapeDtypeStruct((batch + units // 2 * rows, max(out_width, STACK * LANES)), F32),
            jax.ShapeDtypeStruct((rows, half), BF16),
        ),
        (
            jnp.stack([lax.axis_index("yhi"), lax.axis_index("z"), core]),
            sums,
            turned,
            mine,
            theirs,
            order,
            back,
            weight,
            pltpu.with_memory_space_constraint(old_all, pltpu.HBM),
        ),
        flops=0,
        vmem=20,
        in_specs=[smem] + [vmem] * 7 + [pl.BlockSpec(memory_space=pltpu.HBM)],
        scratch_shapes=[
            pltpu.VMEM((nz, 2 * size, LANES), BF16),
            pltpu.VMEM((STACK * KEEP * stride, LANES), F32),
            pltpu.VMEM((STACK, out_width // LANES, KEEP * units, LANES), F32),
            pltpu.VMEM((2, 2 * STACK * GROUP, out_width), BF16),
            pltpu.SemaphoreType.DMA((2, units // 2 + 1)),
        ],
    )
    projected, new_weight = call(
        finish_kernel,
        (jax.ShapeDtypeStruct((batch, out_width), BF16), jax.ShapeDtypeStruct((rows, width), BF16)),
        (core_ref, here, swap(there, "core"), own_new),
        flops=0,
        in_specs=[smem, vmem, vmem, vmem],
    )
    return new_weight, new_momentum[None], projected


def run(sizes, devices):
    fine = Mesh(devices.reshape(sizes), AXES)
    rep, fsdp = AXES[:3], AXES[3:]
    return jax.shard_map(
        functools.partial(body, sizes),
        mesh=fine,
        in_specs=(P(AXES, None), P(rep, fsdp, None), P(rep, fsdp, None), P(fsdp, None), P(fsdp, None, None)),
        out_specs=(P(fsdp, None), P(rep, fsdp, None), P(AXES, None)),
        check_vma=False,
    )


def solution(mesh):
    return run((8, 4, 2, 2, 8), mesh.devices)
```

```python
import functools
import math

import jax
import jax.numpy as jnp
import numpy as np
from jax import lax
from jax.experimental import pallas as pl
from jax.experimental.pallas import tpu as pltpu
from jax.sharding import Mesh
from jax.sharding import PartitionSpec as P

GROUP = 64
KEEP = 8
LANES = 128
STACK = 4
HIGHEST = lax.Precision.HIGHEST
STEP = 0.01
DECAY = 0.1
AXES = ("x", "ylo", "core", "yhi", "z")
F32 = jnp.float32
BF16 = jnp.bfloat16
NT = (((1,), (1,)), ((), ()))
NN = (((1,), (0,)), ((), ()))
TN = (((0,), (0,)), ((), ()))


def basis_pair():
    k = np.arange(GROUP)[:, None]
    n = np.arange(GROUP)[None, :]
    scale = np.where(k == 0, math.sqrt(1.0 / GROUP), math.sqrt(2.0 / GROUP))
    table = scale * np.cos(np.pi * (n + 0.5) * k / GROUP)
    return np.kron(np.eye(2), table).astype(np.float32)


def call(kernel, out_shape, args, flops, vmem=12, **kw):
    return pl.pallas_call(
        kernel,
        out_shape=out_shape,
        compiler_params=pltpu.CompilerParams(vmem_limit_bytes=vmem * 1024 * 1024),
        cost_estimate=pl.CostEstimate(flops=flops, bytes_accessed=0, transcendentals=0),
        **kw,
    )(*args)


def to_all(x, axes, parts):
    copies = lax.optimization_barrier(jnp.broadcast_to(x[None], (parts,) + x.shape))
    return lax.all_to_all(copies, axes, 0, 0, tiled=True)


def pick(sources, rows):
    lane = lax.broadcasted_iota(jnp.int32, sources[0][0].shape, 1) // rows
    merged = None
    for s, (block, group) in enumerate(sources):
        moved = block
        if group != s:
            moved = pltpu.roll(block, ((s - group) % len(sources)) * rows, axis=1)
        merged = moved if merged is None else jnp.where(lane == s, moved, merged)
    return merged


def regroup(blocks, rows, target):
    return pick([(block, target) for block in blocks], rows)


def split(x, axis, order):
    high = x.astype(BF16)
    low = (x - high.astype(F32)).astype(BF16)
    return jnp.concatenate([high, low, high] if order else [high, high, low], axis=axis)


def join_kernel(units, core, weight, idx, out):
    rows, width = weight.shape
    tiles = width // 2 // LANES
    for c in range(tiles):
        at = pl.multiple_of(core[0] * (width // 2) + c * LANES, LANES)
        out[c * rows : (c + 1) * rows, :] = weight[:, pl.ds(at, LANES)]
    total_units = idx.shape[0] // KEEP
    block = [idx[pl.ds(core[0] * units + u, KEEP, stride=total_units), :].astype(F32) for u in range(units)]
    full = units // STACK
    parts = []
    for r in range(full):
        for t in range(STACK):
            parts.append(regroup(block[r * STACK : (r + 1) * STACK], rows, t))
    if full * STACK < units:
        for t in range(0, STACK, 2):
            parts.append(pick([(block[full * STACK + s % 2], t + s // 2) for s in range(STACK)], rows))
    out[tiles * rows :, :] = jnp.concatenate(parts, axis=0).astype(BF16)


def local_kernel(cores, mom, grad, idx, b2, kept, new_mom, kept_wide):
    rows = mom.shape[0]
    total_units = idx.shape[0] // KEEP
    units = total_units // cores
    deep = kept_wide.shape[1]
    forward = split(b2[...], 1, False)
    back = split(b2[...], 0, False)
    freq = lax.broadcasted_iota(jnp.int32, (GROUP, LANES), 0)
    kept_wide[...] = jnp.zeros_like(kept_wide)
    for g in range(total_units // 2):
        tiles = []
        for t in range(STACK):
            cols = pl.ds((STACK * g + t) * LANES, LANES)
            tiles.append(0.9 * mom[:, cols] + grad[:, cols].astype(F32))
        block = jnp.concatenate(tiles, axis=0)
        spec = lax.dot_general(forward, split(block, 1, True), NT, preferred_element_type=F32)
        parts = []
        for c2 in range(2):
            whole = 2 * g + c2
            core, u = whole // units, whole % units
            half = spec[c2 * GROUP : (c2 + 1) * GROUP]
            sent = jnp.zeros_like(half)
            for j in range(KEEP):
                line = j * total_units + whole
                one = jnp.where(freq == idx[line : line + 1, :], half, 0.0)
                at = core * KEEP + j
                kept_wide[u % STACK, u // STACK, at : at + 1, :] = jnp.sum(one, axis=0, keepdims=True)
                sent = sent + one
            parts.append(sent)
        sent = lax.dot_general(split(jnp.concatenate(parts, axis=0), 0, True), back, TN, preferred_element_type=F32)
        rest = block - sent
        for t in range(STACK):
            new_mom[:, pl.ds((STACK * g + t) * LANES, LANES)] = rest[t * rows : (t + 1) * rows]
    both = cores * KEEP
    for ur in range(deep):
        for t in range(STACK):
            lines = pl.ds(t * both * deep + ur, both, stride=deep)
            kept[lines, :] = regroup([kept_wide[b, ur] for b in range(STACK)], rows, t)


def weight_kernel(core, tot, idx, b2, old, new, tot_wide):
    rows, width = new.shape
    deep = tot.shape[0] // (STACK * KEEP)
    span = KEEP * deep
    total_units = idx.shape[0] // KEEP
    units = 2 * width // (STACK * LANES)
    for b in range(STACK):
        tot_wide[b] = regroup([tot[t * span : (t + 1) * span, :] for t in range(STACK)], rows, b)
    freq = lax.broadcasted_iota(jnp.int32, (GROUP, LANES), 0)
    for g in range(units // 2):
        parts = []
        for c2 in range(2):
            u = 2 * g + c2
            value = tot_wide[u % STACK, pl.ds(u // STACK, KEEP, stride=deep), :]
            where = idx[pl.ds(core[0] * units + u, KEEP, stride=total_units), :]
            power = jnp.sum(value * value, axis=0, keepdims=True)
            value = value * lax.rsqrt(power / GROUP + 1e-06)
            spec = jnp.zeros((GROUP, LANES), F32)
            for j in range(KEEP):
                spec = jnp.where(freq == where[j : j + 1], value[j : j + 1], spec)
            parts.append(spec)
        direction = lax.dot_general(
            split(jnp.concatenate(parts, axis=0), 0, True), b2[...], TN, preferred_element_type=F32
        )
        for t in range(STACK):
            cols = pl.ds((STACK * g + t) * LANES, LANES)
            at = pl.multiple_of(core[0] * width + (STACK * g + t) * LANES, LANES)
            kept_part = old[:, pl.ds(at, LANES)].astype(F32) * (1.0 - STEP * DECAY)
            new[:, cols] = (kept_part - STEP * direction[t * rows : (t + 1) * rows]).astype(BF16)


def tokens_kernel(mine, theirs, high, low, out):
    batch = mine.shape[0]
    for t in range(mine.shape[1] // LANES):
        cols = pl.ds(t * LANES, LANES)
        x = jnp.concatenate([mine[:, cols], theirs[:, cols]], axis=0)
        y = lax.dot_general(x, high[...], NT, preferred_element_type=F32)
        y = y + lax.dot_general(x, low[...], NT, preferred_element_type=F32)
        out[:, cols] = y.astype(BF16)


def pack_kernel(units, tot, out):
    deep = tot.shape[0] // (STACK * KEEP)
    full = units // STACK
    lane = lax.broadcasted_iota(jnp.int32, (KEEP, LANES), 1)
    blocks = [[tot[pl.ds(t * KEEP * deep + r, KEEP, stride=deep), :] for t in range(STACK)] for r in range(deep)]
    parts = []
    for r in range(full):
        parts += blocks[r]
    if full < deep:
        for t in range(0, STACK, 2):
            upper = pltpu.roll(blocks[full][t + 1], LANES // 2, axis=1)
            parts.append(jnp.where(lane < LANES // 2, blocks[full][t], upper))
    packed = jnp.concatenate(parts, axis=0).astype(BF16)
    for f in range(out.shape[0]):
        out[f] = packed


def old_kernel(rows, units, place, mine, theirs, source, own, other, freqs, weight, sems):
    nz, size, _ = source.shape
    size = size // 2
    shards = 2 * nz
    lines = KEEP * units
    steps = units // 2
    high = STACK * rows
    fold = LANES // rows

    def copy(h, k):
        at = h * size + (steps * high if k == steps else k * high)
        part = pl.ds(at, lines if k == steps else high)
        return pltpu.make_async_copy(source.at[:, part, :], weight.at[:, part, :], sems.at[h, k])

    for k in [steps] + list(range(steps)):
        for h in range(2):
            copy(h, k).start()

    def start_of(y):
        h = place[0] if y == 0 else 1 - place[0]
        return h * size

    for h in range(2):
        copy(h, steps).wait()
    for q in range(shards // fold):
        blocks = []
        for f in range(fold * q, fold * (q + 1)):
            at = pl.multiple_of(start_of(f // nz) + steps * high, 16)
            blocks.append(weight[f % nz, pl.ds(at, lines), :].astype(F32))
        for b in range(STACK):
            freqs[b, q] = regroup(blocks, rows, b)
    depth = 2 * STACK * GROUP
    wide = nz * rows
    for g in range(steps):
        for h in range(2):
            copy(h, g).wait()
        cols = pl.ds(g * depth, depth)
        for y in range(2):
            at = start_of(y) + g * high
            tiles = []
            for c in range(STACK):
                line = pl.multiple_of(at + c * rows, 16)
                tiles.append(jnp.concatenate([weight[z, pl.ds(line, rows), :] for z in range(nz)], axis=0))
            w = jnp.concatenate(tiles, axis=1)
            lanes = pl.ds(y * wide, wide)
            for x, out in ((mine, own), (theirs, other)):
                part = lax.dot_general(x[:, cols], w, NT, preferred_element_type=F32) * (1.0 - STEP * DECAY)
                out[:, lanes] = part if g == 0 else out[:, lanes] + part


def product_kernel(rows, units, sums, tokens, freqs, old_own, old_other, own, other, vals, spec):
    shards, lines, _ = sums.shape
    batch = own.shape[0]
    fold = LANES // rows
    full = units // STACK
    for q in range(shards // fold):
        blocks = [sums[fold * q + f].astype(F32) for f in range(fold)]
        for b in range(STACK):
            vals[b, q] = regroup(blocks, rows, b)
    pack = 16
    freq = lax.broadcasted_iota(jnp.int32, (GROUP, LANES), 0).astype(F32).astype(BF16)
    freq = [freq[k * pack : (k + 1) * pack] for k in range(GROUP // pack)]
    depth = 2 * STACK * GROUP
    for g in range(units // 2):
        slot = g % 2
        for t in range(STACK):
            for c2 in range(2):
                u = 2 * g + c2
                if u // STACK < full:
                    lane, line = u % STACK, (u // STACK * STACK + t) * KEEP
                else:
                    lane, line = 2 * (t % 2) + u % STACK, (full * STACK + t // 2) * KEEP
                for q in range(shards // fold):
                    value = vals[lane, q, line : line + KEEP, :]
                    where = freqs[lane, q, line : line + KEEP, :]
                    power = jnp.sum(value * value, axis=0, keepdims=True)
                    value = value * (lax.rsqrt(power / GROUP + 1e-06) * (-STEP))
                    s = [jnp.zeros((pack, LANES), BF16)] * len(freq)
                    for j in range(KEEP):
                        v = jnp.broadcast_to(value[j : j + 1], (pack, LANES)).astype(BF16)
                        w = jnp.broadcast_to(where[j : j + 1], (pack, LANES)).astype(BF16)
                        s = [jnp.where(f == w, v, old) for f, old in zip(freq, s)]
                    spec[slot, pl.ds((2 * t + c2) * GROUP, GROUP), pl.ds(q * LANES, LANES)] = jnp.concatenate(s, axis=0)
        cols = pl.ds(g * depth, depth)
        for p, (out, old) in enumerate(((own, old_own), (other, old_other))):
            x = tokens[p * batch : (p + 1) * batch, cols]
            part = lax.dot_general(x, spec[slot], NN, preferred_element_type=F32)
            out[...] = part + (old[...] if g == 0 else out[...])


def sides_kernel(core, mine, theirs, new_weight):
    half = mine.shape[1]
    new_weight[:, pl.ds(pl.multiple_of(core[0] * half, LANES), half)] = mine[...]
    new_weight[:, pl.ds(pl.multiple_of((1 - core[0]) * half, LANES), half)] = theirs[...]


def swap(x, axis):
    return lax.ppermute(x, axis, [(0, 1), (1, 0)])


def body(sizes, tokens, momentum, gradient, weight, kept_index):
    nx, nyl, nc, nyh, nz = sizes
    rows, width = weight.shape
    half = width // nc
    groups = width // (STACK * LANES)
    units = groups
    deep = -(-units // STACK)
    shards = nyh * nz
    batch = tokens.shape[0]
    pair = basis_pair()
    high = pair.astype(jnp.bfloat16)
    low = (pair - high.astype(np.float32)).astype(jnp.bfloat16)
    core = lax.axis_index("core")

    order = kept_index.reshape(rows, groups, STACK, 2, KEEP).transpose(4, 1, 3, 2, 0).reshape(KEEP * nc * units, LANES)
    smem = pl.BlockSpec(memory_space=pltpu.SMEM)
    vmem = pl.BlockSpec(memory_space=pltpu.VMEM)
    core_ref = core.reshape(1)
    size = half // LANES * rows + KEEP * units
    near = call(
        functools.partial(join_kernel, units),
        jax.ShapeDtypeStruct((size, LANES), BF16),
        (core_ref, weight, order),
        flops=0,
        in_specs=[smem, vmem, vmem],
    )
    far = swap(near, "yhi")
    kept, new_momentum = call(
        functools.partial(local_kernel, nc),
        (
            jax.ShapeDtypeStruct((nc * STACK * KEEP * deep, LANES), F32),
            jax.ShapeDtypeStruct((rows, width), F32),
        ),
        (momentum[0], gradient[0], order, jnp.asarray(pair)),
        flops=0,
        scratch_shapes=[pltpu.VMEM((STACK, deep, nc * KEEP, LANES), F32)],
    )
    far, _ = lax.optimization_barrier((far, kept))
    duo = jnp.concatenate([near, far], axis=0)

    pieces = lax.all_to_all(kept.reshape(nyl * nc * nx, 1, deep * LANES), ("ylo", "core", "x"), 0, 0, tiled=True)
    pieces, _ = lax.optimization_barrier((pieces, duo))
    old_all = lax.all_gather(duo, "z", axis=0, tiled=False)
    lines = STACK * KEEP * deep
    total = to_all(jnp.sum(pieces, axis=0), ("ylo", "x"), nyl * nx).reshape(lines, LANES)
    copies = call(
        functools.partial(pack_kernel, units),
        jax.ShapeDtypeStruct((shards, KEEP * units, LANES), BF16),
        (total,),
        flops=0,
    )
    sums = lax.all_to_all(copies, ("yhi", "z"), 0, 0, tiled=True)

    own_new = call(
        weight_kernel,
        jax.ShapeDtypeStruct((rows, half), BF16),
        (core_ref, total, order, jnp.asarray(np.concatenate([high, high, low], axis=0)), weight),
        flops=0,
        in_specs=[smem, vmem, vmem, vmem, vmem],
        scratch_shapes=[pltpu.VMEM((STACK, KEEP * deep, LANES), F32)],
    )
    other_new = swap(own_new, "core")
    new_weight = call(
        sides_kernel,
        jax.ShapeDtypeStruct((rows, width), BF16),
        (core_ref, own_new, other_new),
        flops=0,
        in_specs=[smem, vmem, vmem],
    )

    mine = lax.dynamic_slice(tokens, (0, core * half), (batch, half))
    theirs = swap(lax.dynamic_slice(tokens, (0, (1 - core) * half), (batch, half)), "core")
    turned = call(
        tokens_kernel,
        jax.ShapeDtypeStruct((nc * batch, half), BF16),
        (mine, theirs, jnp.asarray(high), jnp.asarray(low)),
        flops=0,
    )
    turned, _ = lax.optimization_barrier((turned, other_new))
    out_width = shards * rows
    part = jax.ShapeDtypeStruct((batch, out_width), F32)
    table = (STACK, out_width // LANES, KEEP * units, LANES)
    old_own, old_other, freqs = call(
        functools.partial(old_kernel, rows, units),
        (part, part, jax.ShapeDtypeStruct(table, F32)),
        (
            lax.axis_index("yhi").reshape(1),
            mine,
            theirs,
            pltpu.with_memory_space_constraint(old_all, pltpu.HBM),
        ),
        flops=0,
        in_specs=[smem, vmem, vmem, pl.BlockSpec(memory_space=pltpu.HBM)],
        scratch_shapes=[pltpu.VMEM((nz, 2 * size, LANES), BF16), pltpu.SemaphoreType.DMA((2, units // 2 + 1))],
    )
    here, there = call(
        functools.partial(product_kernel, rows, units),
        (part, part),
        (sums, turned, freqs, old_own, old_other),
        flops=0,
        scratch_shapes=[pltpu.VMEM(table, F32), pltpu.VMEM((2, 2 * STACK * GROUP, out_width), BF16)],
    )
    projected = (here + swap(there, "core")).astype(BF16)
    return new_weight, new_momentum[None], projected


def run(sizes, devices):
    fine = Mesh(devices.reshape(sizes), AXES)
    rep, fsdp = AXES[:3], AXES[3:]
    return jax.shard_map(
        functools.partial(body, sizes),
        mesh=fine,
        in_specs=(P(AXES, None), P(rep, fsdp, None), P(rep, fsdp, None), P(fsdp, None), P(fsdp, None, None)),
        out_specs=(P(fsdp, None), P(rep, fsdp, None), P(AXES, None)),
        check_vma=False,
    )


def solution(mesh):
    return run((8, 4, 2, 2, 8), mesh.devices)
```

```python
import functools
import math

import jax
import jax.numpy as jnp
import numpy as np
from jax import lax
from jax.experimental import pallas as pl
from jax.experimental.pallas import tpu as pltpu
from jax.sharding import Mesh
from jax.sharding import PartitionSpec as P

GROUP = 64
KEEP = 8
LANES = 128
STACK = 4
HIGHEST = lax.Precision.HIGHEST
STEP = 0.01
DECAY = 0.1
AXES = ("x", "ylo", "core", "yhi", "z")
F32 = jnp.float32
BF16 = jnp.bfloat16
NT = (((1,), (1,)), ((), ()))
NN = (((1,), (0,)), ((), ()))
TN = (((0,), (0,)), ((), ()))


def basis_pair():
    k = np.arange(GROUP)[:, None]
    n = np.arange(GROUP)[None, :]
    scale = np.where(k == 0, math.sqrt(1.0 / GROUP), math.sqrt(2.0 / GROUP))
    table = scale * np.cos(np.pi * (n + 0.5) * k / GROUP)
    return np.kron(np.eye(2), table).astype(np.float32)


def call(kernel, out_shape, args, flops, vmem=12, **kw):
    return pl.pallas_call(
        kernel,
        out_shape=out_shape,
        compiler_params=pltpu.CompilerParams(vmem_limit_bytes=vmem * 1024 * 1024),
        cost_estimate=pl.CostEstimate(flops=flops, bytes_accessed=0, transcendentals=0),
        **kw,
    )(*args)


def to_all(x, axes, parts):
    copies = lax.optimization_barrier(jnp.broadcast_to(x[None], (parts,) + x.shape))
    return lax.all_to_all(copies, axes, 0, 0, tiled=True)


def pick(sources, rows):
    lane = lax.broadcasted_iota(jnp.int32, sources[0][0].shape, 1) // rows
    merged = None
    for s, (block, group) in enumerate(sources):
        moved = block
        if group != s:
            moved = pltpu.roll(block, ((s - group) % len(sources)) * rows, axis=1)
        merged = moved if merged is None else jnp.where(lane == s, moved, merged)
    return merged


def regroup(blocks, rows, target):
    return pick([(block, target) for block in blocks], rows)


def split(x, axis, order):
    high = x.astype(BF16)
    low = (x - high.astype(F32)).astype(BF16)
    return jnp.concatenate([high, low, high] if order else [high, high, low], axis=axis)


def local_kernel(cores, mom, grad, idx, b2, kept, new_mom, kept_wide):
    rows = mom.shape[0]
    total_units = idx.shape[0] // KEEP
    units = total_units // cores
    deep = kept_wide.shape[1]
    forward = split(b2[...], 1, False)
    back = split(b2[...], 0, False)
    freq = lax.broadcasted_iota(jnp.int32, (GROUP, LANES), 0)
    kept_wide[...] = jnp.zeros_like(kept_wide)
    for g in range(total_units // 2):
        tiles = []
        for t in range(STACK):
            cols = pl.ds((STACK * g + t) * LANES, LANES)
            tiles.append(0.9 * mom[:, cols] + grad[:, cols].astype(F32))
        block = jnp.concatenate(tiles, axis=0)
        spec = lax.dot_general(forward, split(block, 1, True), NT, preferred_element_type=F32)
        parts = []
        for c2 in range(2):
            whole = 2 * g + c2
            core, u = whole // units, whole % units
            half = spec[c2 * GROUP : (c2 + 1) * GROUP]
            sent = jnp.zeros_like(half)
            for j in range(KEEP):
                line = j * total_units + whole
                one = jnp.where(freq == idx[line : line + 1, :], half, 0.0)
                at = core * KEEP + j
                kept_wide[u % STACK, u // STACK, at : at + 1, :] = jnp.sum(one, axis=0, keepdims=True)
                sent = sent + one
            parts.append(sent)
        sent = lax.dot_general(split(jnp.concatenate(parts, axis=0), 0, True), back, TN, preferred_element_type=F32)
        rest = block - sent
        for t in range(STACK):
            new_mom[:, pl.ds((STACK * g + t) * LANES, LANES)] = rest[t * rows : (t + 1) * rows]
    both = cores * KEEP
    for ur in range(deep):
        for t in range(STACK):
            lines = pl.ds(t * both * deep + ur, both, stride=deep)
            kept[lines, :] = regroup([kept_wide[b, ur] for b in range(STACK)], rows, t)


def weight_kernel(core, tot, idx, b2, old, new, tot_wide):
    rows, width = new.shape
    deep = tot.shape[0] // (STACK * KEEP)
    span = KEEP * deep
    total_units = idx.shape[0] // KEEP
    units = 2 * width // (STACK * LANES)
    for b in range(STACK):
        tot_wide[b] = regroup([tot[t * span : (t + 1) * span, :] for t in range(STACK)], rows, b)
    freq = lax.broadcasted_iota(jnp.int32, (GROUP, LANES), 0)
    for g in range(units // 2):
        parts = []
        for c2 in range(2):
            u = 2 * g + c2
            value = tot_wide[u % STACK, pl.ds(u // STACK, KEEP, stride=deep), :]
            where = idx[pl.ds(core[0] * units + u, KEEP, stride=total_units), :]
            power = jnp.sum(value * value, axis=0, keepdims=True)
            value = value * lax.rsqrt(power / GROUP + 1e-06)
            spec = jnp.zeros((GROUP, LANES), F32)
            for j in range(KEEP):
                spec = jnp.where(freq == where[j : j + 1], value[j : j + 1], spec)
            parts.append(spec)
        direction = lax.dot_general(
            split(jnp.concatenate(parts, axis=0), 0, True), b2[...], TN, preferred_element_type=F32
        )
        for t in range(STACK):
            cols = pl.ds((STACK * g + t) * LANES, LANES)
            at = pl.multiple_of(core[0] * width + (STACK * g + t) * LANES, LANES)
            kept_part = old[:, pl.ds(at, LANES)].astype(F32) * (1.0 - STEP * DECAY)
            new[:, cols] = (kept_part - STEP * direction[t * rows : (t + 1) * rows]).astype(BF16)


def tokens_kernel(mine, theirs, high, low, out):
    batch = mine.shape[0]
    for t in range(mine.shape[1] // LANES):
        cols = pl.ds(t * LANES, LANES)
        x = jnp.concatenate([mine[:, cols], theirs[:, cols]], axis=0)
        y = lax.dot_general(x, high[...], NT, preferred_element_type=F32)
        y = y + lax.dot_general(x, low[...], NT, preferred_element_type=F32)
        out[:, cols] = y.astype(BF16)


def pack_kernel(units, core, tot, idx, out):
    deep = tot.shape[0] // (STACK * KEEP)
    full = units // STACK
    rows = LANES // STACK
    lane = lax.broadcasted_iota(jnp.int32, (KEEP, LANES), 1)
    blocks = [[tot[pl.ds(t * KEEP * deep + r, KEEP, stride=deep), :] for t in range(STACK)] for r in range(deep)]
    parts = []
    for r in range(full):
        parts += blocks[r]
    if full < deep:
        for t in range(0, STACK, 2):
            upper = pltpu.roll(blocks[full][t + 1], LANES // 2, axis=1)
            parts.append(jnp.where(lane < LANES // 2, blocks[full][t], upper))
    total_units = idx.shape[0] // KEEP
    block = [idx[pl.ds(core[0] * units + u, KEEP, stride=total_units), :].astype(F32) for u in range(units)]
    for r in range(full):
        for t in range(STACK):
            parts.append(regroup(block[r * STACK : (r + 1) * STACK], rows, t))
    if full < deep:
        for t in range(0, STACK, 2):
            parts.append(pick([(block[full * STACK + s % 2], t + s // 2) for s in range(STACK)], rows))
    packed = jnp.concatenate(parts, axis=0).astype(BF16)
    for f in range(out.shape[0]):
        out[f] = packed


def direction_kernel(rows, units, both, tokens, out, acc, vals, freqs, spec, sem):
    shards = both.shape[0]
    lines = both.shape[1] // 2
    fold = LANES // rows
    full = units // STACK
    for q in range(shards // fold):
        blocks = [both[fold * q + f].astype(F32) for f in range(fold)]
        for b in range(STACK):
            vals[b, q] = regroup([x[:lines] for x in blocks], rows, b)
            freqs[b, q] = regroup([x[lines:] for x in blocks], rows, b)
    pack = 16
    freq = lax.broadcasted_iota(jnp.int32, (GROUP, LANES), 0).astype(F32).astype(BF16)
    freq = [freq[k * pack : (k + 1) * pack] for k in range(GROUP // pack)]
    depth = 2 * STACK * GROUP
    for g in range(units // 2):
        slot = g % 2
        for t in range(STACK):
            for c2 in range(2):
                u = 2 * g + c2
                if u // STACK < full:
                    lane, line = u % STACK, (u // STACK * STACK + t) * KEEP
                else:
                    lane, line = 2 * (t % 2) + u % STACK, (full * STACK + t // 2) * KEEP
                for q in range(shards // fold):
                    value = vals[lane, q, line : line + KEEP, :]
                    where = freqs[lane, q, line : line + KEEP, :]
                    power = jnp.sum(value * value, axis=0, keepdims=True)
                    value = value * (lax.rsqrt(power / GROUP + 1e-06) * (-STEP))
                    s = [jnp.zeros((pack, LANES), BF16)] * len(freq)
                    for j in range(KEEP):
                        v = jnp.broadcast_to(value[j : j + 1], (pack, LANES)).astype(BF16)
                        w = jnp.broadcast_to(where[j : j + 1], (pack, LANES)).astype(BF16)
                        s = [jnp.where(f == w, v, old) for f, old in zip(freq, s)]
                    spec[slot, pl.ds((2 * t + c2) * GROUP, GROUP), pl.ds(q * LANES, LANES)] = jnp.concatenate(s, axis=0)
        part = lax.dot_general(
            tokens[:, pl.ds(g * depth, depth)], spec[slot], NN, preferred_element_type=F32
        )
        acc[...] = part if g == 0 else acc[...] + part
    done = pltpu.make_async_copy(acc, out, sem)
    done.start()
    done.wait()


def old_kernel(rows, place, mine, theirs, source, change, own, other, weight, added, sems):
    nz, _, width = source.shape
    step = STACK * LANES
    wide = nz * rows

    def copy(k):
        cols = pl.ds(k * step, step)
        return pltpu.make_async_copy(source.at[:, :, cols], weight.at[:, :, cols], sems.at[k])

    steps = width // step
    batch = mine.shape[0]
    for k in range(steps):
        copy(k).start()
    rest = pltpu.make_async_copy(change, added, sems.at[steps])
    rest.start()
    for k in range(width // step):
        copy(k).wait()
        cols = pl.ds(k * step, step)
        for y in range(2):
            h = place[0] if y == 0 else 1 - place[0]
            lines = pl.ds(pl.multiple_of(h * rows, 16), rows)
            w = jnp.concatenate([weight[z, lines, cols] for z in range(nz)], axis=0)
            lanes = pl.ds(y * wide, wide)
            for x, out in ((mine, own), (theirs, other)):
                part = lax.dot_general(x[:, cols], w, NT, preferred_element_type=F32) * (1.0 - STEP * DECAY)
                out[:, lanes] = part if k == 0 else out[:, lanes] + part
    rest.wait()
    own[...] += added[:batch, :]
    other[...] += added[batch:, :]


def sides_kernel(core, mine, theirs, new_weight):
    half = mine.shape[1]
    new_weight[:, pl.ds(pl.multiple_of(core[0] * half, LANES), half)] = mine[...]
    new_weight[:, pl.ds(pl.multiple_of((1 - core[0]) * half, LANES), half)] = theirs[...]


def swap(x, axis):
    return lax.ppermute(x, axis, [(0, 1), (1, 0)])


def body(sizes, tokens, momentum, gradient, weight, kept_index):
    nx, nyl, nc, nyh, nz = sizes
    rows, width = weight.shape
    half = width // nc
    groups = width // (STACK * LANES)
    units = groups
    deep = -(-units // STACK)
    shards = nyh * nz
    batch = tokens.shape[0]
    pair = basis_pair()
    high = pair.astype(jnp.bfloat16)
    low = (pair - high.astype(np.float32)).astype(jnp.bfloat16)
    core = lax.axis_index("core")

    near = lax.dynamic_slice(weight, (0, core * half), (rows, half))
    far = swap(near, "yhi")
    order = kept_index.reshape(rows, groups, STACK, 2, KEEP).transpose(4, 1, 3, 2, 0).reshape(KEEP * nc * units, LANES)
    smem = pl.BlockSpec(memory_space=pltpu.SMEM)
    vmem = pl.BlockSpec(memory_space=pltpu.VMEM)
    core_ref = core.reshape(1)
    kept, new_momentum = call(
        functools.partial(local_kernel, nc),
        (
            jax.ShapeDtypeStruct((nc * STACK * KEEP * deep, LANES), F32),
            jax.ShapeDtypeStruct((rows, width), F32),
        ),
        (momentum[0], gradient[0], order, jnp.asarray(pair)),
        flops=0,
        scratch_shapes=[pltpu.VMEM((STACK, deep, nc * KEEP, LANES), F32)],
    )
    far, _ = lax.optimization_barrier((far, kept))
    duo = jnp.concatenate([near, far], axis=0)

    pieces = lax.all_to_all(kept.reshape(nyl * nc * nx, 1, deep * LANES), ("ylo", "core", "x"), 0, 0, tiled=True)
    pieces, _ = lax.optimization_barrier((pieces, duo))
    old_all = lax.all_gather(duo, "z", axis=0, tiled=False)
    lines = STACK * KEEP * deep
    total = to_all(jnp.sum(pieces, axis=0), ("ylo", "x"), nyl * nx).reshape(lines, LANES)
    copies = call(
        functools.partial(pack_kernel, units),
        jax.ShapeDtypeStruct((shards, 2 * KEEP * units, LANES), BF16),
        (core_ref, total, order),
        flops=20_000_000_000,
        in_specs=[smem, vmem, vmem],
    )
    both = lax.all_to_all(copies, ("yhi", "z"), 0, 0, tiled=True)

    own_new = call(
        weight_kernel,
        jax.ShapeDtypeStruct((rows, half), BF16),
        (core_ref, total, order, jnp.asarray(np.concatenate([high, high, low], axis=0)), weight),
        flops=0,
        in_specs=[smem, vmem, vmem, vmem, vmem],
        scratch_shapes=[pltpu.VMEM((STACK, KEEP * deep, LANES), F32)],
    )
    other_new = swap(own_new, "core")
    new_weight = call(
        sides_kernel,
        jax.ShapeDtypeStruct((rows, width), BF16),
        (core_ref, own_new, other_new),
        flops=0,
        in_specs=[smem, vmem, vmem],
    )

    mine = lax.dynamic_slice(tokens, (0, core * half), (batch, half))
    theirs = swap(lax.dynamic_slice(tokens, (0, (1 - core) * half), (batch, half)), "core")
    turned = call(
        tokens_kernel,
        jax.ShapeDtypeStruct((nc * batch, half), BF16),
        (mine, theirs, jnp.asarray(high), jnp.asarray(low)),
        flops=0,
    )
    turned, _ = lax.optimization_barrier((turned, other_new))
    out_width = shards * rows
    part = jax.ShapeDtypeStruct((batch, out_width), F32)
    table = pltpu.VMEM((STACK, out_width // LANES, KEEP * units, LANES), F32)
    hbm = pl.BlockSpec(memory_space=pltpu.HBM)
    whole = pltpu.VMEM((nc * batch, out_width), F32)
    change = call(
        functools.partial(direction_kernel, rows, units),
        pltpu.HBM((nc * batch, out_width), F32),
        (both, turned),
        flops=0,
        out_specs=hbm,
        scratch_shapes=[
            whole,
            table,
            table,
            pltpu.VMEM((2, 2 * STACK * GROUP, out_width), BF16),
            pltpu.SemaphoreType.DMA(()),
        ],
    )
    here, there = call(
        functools.partial(old_kernel, rows),
        (part, part),
        (
            lax.axis_index("yhi").reshape(1),
            mine,
            theirs,
            pltpu.with_memory_space_constraint(old_all, pltpu.HBM),
            pltpu.with_memory_space_constraint(change, pltpu.HBM),
        ),
        flops=0,
        in_specs=[smem, vmem, vmem, hbm, hbm],
        scratch_shapes=[
            pltpu.VMEM((nz, 2 * rows, half), BF16),
            whole,
            pltpu.SemaphoreType.DMA((half // (STACK * LANES) + 1,)),
        ],
    )
    projected = (here + swap(there, "core")).astype(BF16)
    return new_weight, new_momentum[None], projected


def run(sizes, devices):
    fine = Mesh(devices.reshape(sizes), AXES)
    rep, fsdp = AXES[:3], AXES[3:]
    return jax.shard_map(
        functools.partial(body, sizes),
        mesh=fine,
        in_specs=(P(AXES, None), P(rep, fsdp, None), P(rep, fsdp, None), P(fsdp, None), P(fsdp, None, None)),
        out_specs=(P(fsdp, None), P(rep, fsdp, None), P(AXES, None)),
        check_vma=False,
    )


def solution(mesh):
    return run((8, 4, 2, 2, 8), mesh.devices)
```

```python
import functools
import math

import jax
import jax.numpy as jnp
import numpy as np
from jax import lax
from jax.experimental import pallas as pl
from jax.experimental.pallas import tpu as pltpu
from jax.sharding import Mesh
from jax.sharding import PartitionSpec as P

GROUP = 64
KEEP = 8
LANES = 128
STACK = 4
HIGHEST = lax.Precision.HIGHEST
STEP = 0.01
DECAY = 0.1
AXES = ("x", "ylo", "core", "yhi", "z")
F32 = jnp.float32
BF16 = jnp.bfloat16
NT = (((1,), (1,)), ((), ()))
NN = (((1,), (0,)), ((), ()))
TN = (((0,), (0,)), ((), ()))


def basis_pair():
    k = np.arange(GROUP)[:, None]
    n = np.arange(GROUP)[None, :]
    scale = np.where(k == 0, math.sqrt(1.0 / GROUP), math.sqrt(2.0 / GROUP))
    table = scale * np.cos(np.pi * (n + 0.5) * k / GROUP)
    return np.kron(np.eye(2), table).astype(np.float32)


def call(kernel, out_shape, args, flops, vmem=12, **kw):
    return pl.pallas_call(
        kernel,
        out_shape=out_shape,
        compiler_params=pltpu.CompilerParams(vmem_limit_bytes=vmem * 1024 * 1024),
        cost_estimate=pl.CostEstimate(flops=flops, bytes_accessed=0, transcendentals=0),
        **kw,
    )(*args)


def to_all(x, axes, parts):
    copies = lax.optimization_barrier(jnp.broadcast_to(x[None], (parts,) + x.shape))
    return lax.all_to_all(copies, axes, 0, 0, tiled=True)


def pick(sources, rows):
    lane = lax.broadcasted_iota(jnp.int32, sources[0][0].shape, 1) // rows
    merged = None
    for s, (block, group) in enumerate(sources):
        moved = block
        if group != s:
            moved = pltpu.roll(block, ((s - group) % len(sources)) * rows, axis=1)
        merged = moved if merged is None else jnp.where(lane == s, moved, merged)
    return merged


def regroup(blocks, rows, target):
    return pick([(block, target) for block in blocks], rows)


def split(x, axis, order):
    high = x.astype(BF16)
    low = (x - high.astype(F32)).astype(BF16)
    return jnp.concatenate([high, low, high] if order else [high, high, low], axis=axis)


def join_kernel(units, core, weight, idx, out):
    rows, width = weight.shape
    tiles = width // 2 // LANES
    for c in range(tiles):
        at = pl.multiple_of(core[0] * (width // 2) + c * LANES, LANES)
        out[c * rows : (c + 1) * rows, :] = weight[:, pl.ds(at, LANES)]
    total_units = idx.shape[0] // KEEP
    block = [idx[pl.ds(core[0] * units + u, KEEP, stride=total_units), :].astype(F32) for u in range(units)]
    full = units // STACK
    parts = []
    for r in range(full):
        for t in range(STACK):
            parts.append(regroup(block[r * STACK : (r + 1) * STACK], rows, t))
    if full * STACK < units:
        for t in range(0, STACK, 2):
            parts.append(pick([(block[full * STACK + s % 2], t + s // 2) for s in range(STACK)], rows))
    out[tiles * rows :, :] = jnp.concatenate(parts, axis=0).astype(BF16)


def local_kernel(cores, mom, grad, idx, b2, kept, new_mom, kept_wide):
    rows = mom.shape[0]
    total_units = idx.shape[0] // KEEP
    units = total_units // cores
    deep = kept_wide.shape[1]
    forward = split(b2[...], 1, False)
    back = split(b2[...], 0, False)
    freq = lax.broadcasted_iota(jnp.int32, (GROUP, LANES), 0)
    kept_wide[...] = jnp.zeros_like(kept_wide)
    for g in range(total_units // 2):
        tiles = []
        for t in range(STACK):
            cols = pl.ds((STACK * g + t) * LANES, LANES)
            tiles.append(0.9 * mom[:, cols] + grad[:, cols].astype(F32))
        block = jnp.concatenate(tiles, axis=0)
        spec = lax.dot_general(forward, split(block, 1, True), NT, preferred_element_type=F32)
        parts = []
        for c2 in range(2):
            whole = 2 * g + c2
            core, u = whole // units, whole % units
            half = spec[c2 * GROUP : (c2 + 1) * GROUP]
            sent = jnp.zeros_like(half)
            for j in range(KEEP):
                line = j * total_units + whole
                one = jnp.where(freq == idx[line : line + 1, :], half, 0.0)
                at = core * KEEP + j
                kept_wide[u % STACK, u // STACK, at : at + 1, :] = jnp.sum(one, axis=0, keepdims=True)
                sent = sent + one
            parts.append(sent)
        sent = lax.dot_general(split(jnp.concatenate(parts, axis=0), 0, True), back, TN, preferred_element_type=F32)
        rest = block - sent
        for t in range(STACK):
            new_mom[:, pl.ds((STACK * g + t) * LANES, LANES)] = rest[t * rows : (t + 1) * rows]
    both = cores * KEEP
    for ur in range(deep):
        for t in range(STACK):
            lines = pl.ds(t * both * deep + ur, both, stride=deep)
            kept[lines, :] = regroup([kept_wide[b, ur] for b in range(STACK)], rows, t)


def weight_kernel(core, tot, idx, b2, old, new, tot_wide):
    rows, width = new.shape
    deep = tot.shape[0] // (STACK * KEEP)
    span = KEEP * deep
    total_units = idx.shape[0] // KEEP
    units = 2 * width // (STACK * LANES)
    for b in range(STACK):
        tot_wide[b] = regroup([tot[t * span : (t + 1) * span, :] for t in range(STACK)], rows, b)
    freq = lax.broadcasted_iota(jnp.int32, (GROUP, LANES), 0)
    for g in range(units // 2):
        parts = []
        for c2 in range(2):
            u = 2 * g + c2
            value = tot_wide[u % STACK, pl.ds(u // STACK, KEEP, stride=deep), :]
            where = idx[pl.ds(core[0] * units + u, KEEP, stride=total_units), :]
            power = jnp.sum(value * value, axis=0, keepdims=True)
            value = value * lax.rsqrt(power / GROUP + 1e-06)
            spec = jnp.zeros((GROUP, LANES), F32)
            for j in range(KEEP):
                spec = jnp.where(freq == where[j : j + 1], value[j : j + 1], spec)
            parts.append(spec)
        direction = lax.dot_general(
            split(jnp.concatenate(parts, axis=0), 0, True), b2[...], TN, preferred_element_type=F32
        )
        for t in range(STACK):
            cols = pl.ds((STACK * g + t) * LANES, LANES)
            at = pl.multiple_of(core[0] * width + (STACK * g + t) * LANES, LANES)
            kept_part = old[:, pl.ds(at, LANES)].astype(F32) * (1.0 - STEP * DECAY)
            new[:, cols] = (kept_part - STEP * direction[t * rows : (t + 1) * rows]).astype(BF16)


def tokens_kernel(mine, theirs, high, low, out):
    batch = mine.shape[0]
    for t in range(mine.shape[1] // LANES):
        cols = pl.ds(t * LANES, LANES)
        x = jnp.concatenate([mine[:, cols], theirs[:, cols]], axis=0)
        y = lax.dot_general(x, high[...], NT, preferred_element_type=F32)
        y = y + lax.dot_general(x, low[...], NT, preferred_element_type=F32)
        out[:, cols] = y.astype(BF16)


def pack_kernel(units, tot, out):
    deep = tot.shape[0] // (STACK * KEEP)
    full = units // STACK
    lane = lax.broadcasted_iota(jnp.int32, (KEEP, LANES), 1)
    blocks = [[tot[pl.ds(t * KEEP * deep + r, KEEP, stride=deep), :] for t in range(STACK)] for r in range(deep)]
    parts = []
    for r in range(full):
        parts += blocks[r]
    if full < deep:
        for t in range(0, STACK, 2):
            upper = pltpu.roll(blocks[full][t + 1], LANES // 2, axis=1)
            parts.append(jnp.where(lane < LANES // 2, blocks[full][t], upper))
    packed = jnp.concatenate(parts, axis=0).astype(BF16)
    for f in range(out.shape[0]):
        out[f] = packed


def product_kernel(rows, units, place, sums, tokens, mine, theirs, source, own, other, weight, vals, freqs, spec, sems):
    shards, lines, _ = sums.shape
    nz, size, _ = source.shape
    size = size // 2
    steps = units // 2
    high = STACK * rows
    fold = LANES // rows
    full = units // STACK

    def copy(h, k):
        at = h * size + (steps * high if k == steps else k * high)
        part = pl.ds(at, lines if k == steps else high)
        return pltpu.make_async_copy(source.at[:, part, :], weight.at[:, part, :], sems.at[h, k])

    for k in [steps] + list(range(steps)):
        for h in range(2):
            copy(h, k).start()

    def start_of(y):
        h = place[0] if y == 0 else 1 - place[0]
        return h * size

    def spread(blocks, out, q):
        for b in range(STACK):
            out[b, q] = regroup(blocks, rows, b)

    for q in range(shards // fold):
        spread([sums[fold * q + f].astype(F32) for f in range(fold)], vals, q)
    for h in range(2):
        copy(h, steps).wait()
    for q in range(shards // fold):
        blocks = []
        for f in range(fold * q, fold * (q + 1)):
            at = pl.multiple_of(start_of(f // nz) + steps * high, 16)
            blocks.append(weight[f % nz, pl.ds(at, lines), :].astype(F32))
        spread(blocks, freqs, q)
    pack = 16
    freq = lax.broadcasted_iota(jnp.int32, (GROUP, LANES), 0).astype(F32).astype(BF16)
    freq = [freq[k * pack : (k + 1) * pack] for k in range(GROUP // pack)]
    depth = 2 * STACK * GROUP
    batch = mine.shape[0]
    wide = nz * rows
    for g in range(steps):
        slot = g % 2
        for t in range(STACK):
            for c2 in range(2):
                u = 2 * g + c2
                if u // STACK < full:
                    lane, line = u % STACK, (u // STACK * STACK + t) * KEEP
                else:
                    lane, line = 2 * (t % 2) + u % STACK, (full * STACK + t // 2) * KEEP
                for q in range(shards // fold):
                    cols = pl.ds(q * LANES, LANES)
                    value = vals[lane, q, line : line + KEEP, :]
                    where = freqs[lane, q, line : line + KEEP, :]
                    power = jnp.sum(value * value, axis=0, keepdims=True)
                    value = value * (lax.rsqrt(power / GROUP + 1e-06) * (-STEP))
                    s = [jnp.zeros((pack, LANES), BF16)] * len(freq)
                    for j in range(KEEP):
                        v = jnp.broadcast_to(value[j : j + 1], (pack, LANES)).astype(BF16)
                        w = jnp.broadcast_to(where[j : j + 1], (pack, LANES)).astype(BF16)
                        s = [jnp.where(f == w, v, old) for f, old in zip(freq, s)]
                    spec[slot, pl.ds((2 * t + c2) * GROUP, GROUP), cols] = jnp.concatenate(s, axis=0)
        for h in range(2):
            copy(h, g).wait()
        cols = pl.ds(g * depth, depth)
        for y in range(2):
            at = start_of(y) + g * high
            tiles = []
            for c in range(STACK):
                line = pl.multiple_of(at + c * rows, 16)
                tiles.append(jnp.concatenate([weight[z, pl.ds(line, rows), :] for z in range(nz)], axis=0))
            w = jnp.concatenate(tiles, axis=1)
            lanes = pl.ds(y * wide, wide)
            for p, (x, out) in enumerate(((mine, own), (theirs, other))):
                part = lax.dot_general(x[:, cols], w, NT, preferred_element_type=F32) * (1.0 - STEP * DECAY)
                part += lax.dot_general(
                    tokens[p * batch : (p + 1) * batch, cols], spec[slot, :, lanes], NN, preferred_element_type=F32
                )
                out[:, lanes] = part if g == 0 else out[:, lanes] + part


def sides_kernel(core, mine, theirs, new_weight):
    half = mine.shape[1]
    new_weight[:, pl.ds(pl.multiple_of(core[0] * half, LANES), half)] = mine[...]
    new_weight[:, pl.ds(pl.multiple_of((1 - core[0]) * half, LANES), half)] = theirs[...]


def swap(x, axis):
    return lax.ppermute(x, axis, [(0, 1), (1, 0)])


def body(sizes, tokens, momentum, gradient, weight, kept_index):
    nx, nyl, nc, nyh, nz = sizes
    rows, width = weight.shape
    half = width // nc
    groups = width // (STACK * LANES)
    units = groups
    deep = -(-units // STACK)
    shards = nyh * nz
    batch = tokens.shape[0]
    pair = basis_pair()
    high = pair.astype(jnp.bfloat16)
    low = (pair - high.astype(np.float32)).astype(jnp.bfloat16)
    core = lax.axis_index("core")

    order = kept_index.reshape(rows, groups, STACK, 2, KEEP).transpose(4, 1, 3, 2, 0).reshape(KEEP * nc * units, LANES)
    smem = pl.BlockSpec(memory_space=pltpu.SMEM)
    vmem = pl.BlockSpec(memory_space=pltpu.VMEM)
    core_ref = core.reshape(1)
    size = half // LANES * rows + KEEP * units
    near = call(
        functools.partial(join_kernel, units),
        jax.ShapeDtypeStruct((size, LANES), BF16),
        (core_ref, weight, order),
        flops=0,
        in_specs=[smem, vmem, vmem],
    )
    far = swap(near, "yhi")
    kept, new_momentum = call(
        functools.partial(local_kernel, nc),
        (
            jax.ShapeDtypeStruct((nc * STACK * KEEP * deep, LANES), F32),
            jax.ShapeDtypeStruct((rows, width), F32),
        ),
        (momentum[0], gradient[0], order, jnp.asarray(pair)),
        flops=0,
        scratch_shapes=[pltpu.VMEM((STACK, deep, nc * KEEP, LANES), F32)],
    )
    far, _ = lax.optimization_barrier((far, kept))
    duo = jnp.concatenate([near, far], axis=0)

    pieces = lax.all_to_all(kept.reshape(nyl * nc * nx, 1, deep * LANES), ("ylo", "core", "x"), 0, 0, tiled=True)
    pieces, _ = lax.optimization_barrier((pieces, duo))
    old_all = lax.all_gather(duo, "z", axis=0, tiled=False)
    lines = STACK * KEEP * deep
    total = to_all(jnp.sum(pieces, axis=0), ("ylo", "x"), nyl * nx).reshape(lines, LANES)
    copies = call(
        functools.partial(pack_kernel, units),
        jax.ShapeDtypeStruct((shards, KEEP * units, LANES), BF16),
        (total,),
        flops=0,
    )
    sums = lax.all_to_all(copies, ("yhi", "z"), 0, 0, tiled=True)

    own_new = call(
        weight_kernel,
        jax.ShapeDtypeStruct((rows, half), BF16),
        (core_ref, total, order, jnp.asarray(np.concatenate([high, high, low], axis=0)), weight),
        flops=0,
        in_specs=[smem, vmem, vmem, vmem, vmem],
        scratch_shapes=[pltpu.VMEM((STACK, KEEP * deep, LANES), F32)],
    )
    other_new = swap(own_new, "core")
    new_weight = call(
        sides_kernel,
        jax.ShapeDtypeStruct((rows, width), BF16),
        (core_ref, own_new, other_new),
        flops=0,
        in_specs=[smem, vmem, vmem],
    )

    mine = lax.dynamic_slice(tokens, (0, core * half), (batch, half))
    theirs = swap(lax.dynamic_slice(tokens, (0, (1 - core) * half), (batch, half)), "core")
    turned = call(
        tokens_kernel,
        jax.ShapeDtypeStruct((nc * batch, half), BF16),
        (mine, theirs, jnp.asarray(high), jnp.asarray(low)),
        flops=0,
    )
    turned, _ = lax.optimization_barrier((turned, other_new))
    out_width = shards * rows
    part = jax.ShapeDtypeStruct((batch, out_width), F32)
    table = pltpu.VMEM((STACK, out_width // LANES, KEEP * units, LANES), F32)
    here, there = call(
        functools.partial(product_kernel, rows, units),
        (part, part),
        (
            lax.axis_index("yhi").reshape(1),
            sums,
            turned,
            mine,
            theirs,
            pltpu.with_memory_space_constraint(old_all, pltpu.HBM),
        ),
        flops=0,
        vmem=20,
        in_specs=[smem, vmem, vmem, vmem, vmem, pl.BlockSpec(memory_space=pltpu.HBM)],
        scratch_shapes=[
            pltpu.VMEM((nz, 2 * size, LANES), BF16),
            table,
            table,
            pltpu.VMEM((2, 2 * STACK * GROUP, out_width), BF16),
            pltpu.SemaphoreType.DMA((2, units // 2 + 1)),
        ],
    )
    projected = (here + swap(there, "core")).astype(BF16)
    return new_weight, new_momentum[None], projected


def run(sizes, devices):
    fine = Mesh(devices.reshape(sizes), AXES)
    rep, fsdp = AXES[:3], AXES[3:]
    return jax.shard_map(
        functools.partial(body, sizes),
        mesh=fine,
        in_specs=(P(AXES, None), P(rep, fsdp, None), P(rep, fsdp, None), P(fsdp, None), P(fsdp, None, None)),
        out_specs=(P(fsdp, None), P(rep, fsdp, None), P(AXES, None)),
        check_vma=False,
    )


def solution(mesh):
    return run((8, 4, 2, 2, 8), mesh.devices)
```

```python
import functools
import math

import jax
import jax.numpy as jnp
import numpy as np
from jax import lax
from jax.experimental import pallas as pl
from jax.experimental.pallas import tpu as pltpu
from jax.sharding import Mesh
from jax.sharding import PartitionSpec as P

GROUP = 64
KEEP = 8
LANES = 128
STACK = 4
HIGHEST = lax.Precision.HIGHEST
STEP = 0.01
DECAY = 0.1
AXES = ("x", "ylo", "core", "yhi", "z")
F32 = jnp.float32
BF16 = jnp.bfloat16
NT = (((1,), (1,)), ((), ()))
NN = (((1,), (0,)), ((), ()))
TN = (((0,), (0,)), ((), ()))


def basis_pair():
    k = np.arange(GROUP)[:, None]
    n = np.arange(GROUP)[None, :]
    scale = np.where(k == 0, math.sqrt(1.0 / GROUP), math.sqrt(2.0 / GROUP))
    table = scale * np.cos(np.pi * (n + 0.5) * k / GROUP)
    return np.kron(np.eye(2), table).astype(np.float32)


def call(kernel, out_shape, args, flops, vmem=12, **kw):
    return pl.pallas_call(
        kernel,
        out_shape=out_shape,
        compiler_params=pltpu.CompilerParams(vmem_limit_bytes=vmem * 1024 * 1024),
        cost_estimate=pl.CostEstimate(flops=flops, bytes_accessed=0, transcendentals=0),
        **kw,
    )(*args)


def to_all(x, axes, parts):
    copies = lax.optimization_barrier(jnp.broadcast_to(x[None], (parts,) + x.shape))
    return lax.all_to_all(copies, axes, 0, 0, tiled=True)


def pick(sources, rows):
    lane = lax.broadcasted_iota(jnp.int32, sources[0][0].shape, 1) // rows
    merged = None
    for s, (block, group) in enumerate(sources):
        moved = block
        if group != s:
            moved = pltpu.roll(block, ((s - group) % len(sources)) * rows, axis=1)
        merged = moved if merged is None else jnp.where(lane == s, moved, merged)
    return merged


def regroup(blocks, rows, target):
    return pick([(block, target) for block in blocks], rows)


def split(x, axis, order):
    high = x.astype(BF16)
    low = (x - high.astype(F32)).astype(BF16)
    return jnp.concatenate([high, low, high] if order else [high, high, low], axis=axis)


def join_kernel(units, core, weight, idx, out):
    rows, width = weight.shape
    tiles = width // 2 // LANES
    for c in range(tiles):
        at = pl.multiple_of(core[0] * (width // 2) + c * LANES, LANES)
        out[c * rows : (c + 1) * rows, :] = weight[:, pl.ds(at, LANES)]
    total_units = idx.shape[0] // KEEP
    block = [idx[pl.ds(core[0] * units + u, KEEP, stride=total_units), :].astype(F32) for u in range(units)]
    full = units // STACK
    parts = []
    for r in range(full):
        for t in range(STACK):
            parts.append(regroup(block[r * STACK : (r + 1) * STACK], rows, t))
    if full * STACK < units:
        for t in range(0, STACK, 2):
            parts.append(pick([(block[full * STACK + s % 2], t + s // 2) for s in range(STACK)], rows))
    out[tiles * rows :, :] = jnp.concatenate(parts, axis=0).astype(BF16)


def local_kernel(cores, mom, grad, idx, b2, kept, new_mom, kept_wide):
    rows = mom.shape[0]
    total_units = idx.shape[0] // KEEP
    units = total_units // cores
    deep = kept_wide.shape[1]
    forward = split(b2[...], 1, False)
    back = split(b2[...], 0, False)
    freq = lax.broadcasted_iota(jnp.int32, (GROUP, LANES), 0)
    kept_wide[...] = jnp.zeros_like(kept_wide)
    for g in range(total_units // 2):
        tiles = []
        for t in range(STACK):
            cols = pl.ds((STACK * g + t) * LANES, LANES)
            tiles.append(0.9 * mom[:, cols] + grad[:, cols].astype(F32))
        block = jnp.concatenate(tiles, axis=0)
        spec = lax.dot_general(forward, split(block, 1, True), NT, preferred_element_type=F32)
        parts = []
        for c2 in range(2):
            whole = 2 * g + c2
            core, u = whole // units, whole % units
            half = spec[c2 * GROUP : (c2 + 1) * GROUP]
            sent = jnp.zeros_like(half)
            for j in range(KEEP):
                line = j * total_units + whole
                one = jnp.where(freq == idx[line : line + 1, :], half, 0.0)
                at = core * KEEP + j
                kept_wide[u % STACK, u // STACK, at : at + 1, :] = jnp.sum(one, axis=0, keepdims=True)
                sent = sent + one
            parts.append(sent)
        sent = lax.dot_general(split(jnp.concatenate(parts, axis=0), 0, True), back, TN, preferred_element_type=F32)
        rest = block - sent
        for t in range(STACK):
            new_mom[:, pl.ds((STACK * g + t) * LANES, LANES)] = rest[t * rows : (t + 1) * rows]
    both = cores * KEEP
    for ur in range(deep):
        for t in range(STACK):
            lines = pl.ds(t * both * deep + ur, both, stride=deep)
            kept[lines, :] = regroup([kept_wide[b, ur] for b in range(STACK)], rows, t)


def weight_kernel(core, tot, idx, b2, old, new, tot_wide):
    rows, width = new.shape
    deep = tot.shape[0] // (STACK * KEEP)
    span = KEEP * deep
    total_units = idx.shape[0] // KEEP
    units = 2 * width // (STACK * LANES)
    for b in range(STACK):
        tot_wide[b] = regroup([tot[t * span : (t + 1) * span, :] for t in range(STACK)], rows, b)
    freq = lax.broadcasted_iota(jnp.int32, (GROUP, LANES), 0)
    for g in range(units // 2):
        parts = []
        for c2 in range(2):
            u = 2 * g + c2
            value = tot_wide[u % STACK, pl.ds(u // STACK, KEEP, stride=deep), :]
            where = idx[pl.ds(core[0] * units + u, KEEP, stride=total_units), :]
            power = jnp.sum(value * value, axis=0, keepdims=True)
            value = value * lax.rsqrt(power / GROUP + 1e-06)
            spec = jnp.zeros((GROUP, LANES), F32)
            for j in range(KEEP):
                spec = jnp.where(freq == where[j : j + 1], value[j : j + 1], spec)
            parts.append(spec)
        direction = lax.dot_general(
            split(jnp.concatenate(parts, axis=0), 0, True), b2[...], TN, preferred_element_type=F32
        )
        for t in range(STACK):
            cols = pl.ds((STACK * g + t) * LANES, LANES)
            at = pl.multiple_of(core[0] * width + (STACK * g + t) * LANES, LANES)
            kept_part = old[:, pl.ds(at, LANES)].astype(F32) * (1.0 - STEP * DECAY)
            new[:, cols] = (kept_part - STEP * direction[t * rows : (t + 1) * rows]).astype(BF16)


def tokens_kernel(mine, theirs, high, low, out):
    batch = mine.shape[0]
    for t in range(mine.shape[1] // LANES):
        cols = pl.ds(t * LANES, LANES)
        x = jnp.concatenate([mine[:, cols], theirs[:, cols]], axis=0)
        y = lax.dot_general(x, high[...], NT, preferred_element_type=F32)
        y = y + lax.dot_general(x, low[...], NT, preferred_element_type=F32)
        out[:, cols] = y.astype(BF16)


def pack_kernel(units, tot, out):
    deep = tot.shape[0] // (STACK * KEEP)
    full = units // STACK
    lane = lax.broadcasted_iota(jnp.int32, (KEEP, LANES), 1)
    blocks = [[tot[pl.ds(t * KEEP * deep + r, KEEP, stride=deep), :] for t in range(STACK)] for r in range(deep)]
    parts = []
    for r in range(full):
        parts += blocks[r]
    if full < deep:
        for t in range(0, STACK, 2):
            upper = pltpu.roll(blocks[full][t + 1], LANES // 2, axis=1)
            parts.append(jnp.where(lane < LANES // 2, blocks[full][t], upper))
    packed = jnp.concatenate(parts, axis=0).astype(BF16)
    for f in range(out.shape[0]):
        out[f] = packed


def product_kernel(rows, units, place, sums, tokens, mine, theirs, source, own, other, weight, vals, freqs, spec, sems):
    shards, lines, _ = sums.shape
    nz, size, _ = source.shape
    size = size // 2
    steps = units // 2
    high = STACK * rows
    fold = LANES // rows
    full = units // STACK

    def copy(h, k):
        at = h * size + (steps * high if k == steps else k * high)
        part = pl.ds(at, lines if k == steps else high)
        return pltpu.make_async_copy(source.at[:, part, :], weight.at[:, part, :], sems.at[h, k])

    for k in [steps] + list(range(steps)):
        for h in range(2):
            copy(h, k).start()

    def start_of(y):
        h = place[0] if y == 0 else 1 - place[0]
        return h * size

    def spread(blocks, out, q):
        for b in range(STACK):
            out[b, q] = regroup(blocks, rows, b)

    for q in range(shards // fold):
        spread([sums[fold * q + f].astype(F32) for f in range(fold)], vals, q)
    for h in range(2):
        copy(h, steps).wait()
    for q in range(shards // fold):
        blocks = []
        for f in range(fold * q, fold * (q + 1)):
            at = pl.multiple_of(start_of(f // nz) + steps * high, 16)
            blocks.append(weight[f % nz, pl.ds(at, lines), :].astype(F32))
        spread(blocks, freqs, q)
    pack = 16
    freq = lax.broadcasted_iota(jnp.int32, (GROUP, LANES), 0).astype(F32).astype(BF16)
    freq = [freq[k * pack : (k + 1) * pack] for k in range(GROUP // pack)]
    depth = 2 * STACK * GROUP
    batch = mine.shape[0]
    wide = nz * rows
    for g in range(steps):
        slot = g % 2
        for t in range(STACK):
            for c2 in range(2):
                u = 2 * g + c2
                if u // STACK < full:
                    lane, line = u % STACK, (u // STACK * STACK + t) * KEEP
                else:
                    lane, line = 2 * (t % 2) + u % STACK, (full * STACK + t // 2) * KEEP
                for q in range(shards // fold):
                    cols = pl.ds(q * LANES, LANES)
                    value = vals[lane, q, line : line + KEEP, :]
                    where = freqs[lane, q, line : line + KEEP, :]
                    power = jnp.sum(value * value, axis=0, keepdims=True)
                    value = value * (lax.rsqrt(power / GROUP + 1e-06) * (-STEP))
                    s = [jnp.zeros((pack, LANES), BF16)] * len(freq)
                    for j in range(KEEP):
                        v = jnp.broadcast_to(value[j : j + 1], (pack, LANES)).astype(BF16)
                        w = jnp.broadcast_to(where[j : j + 1], (pack, LANES)).astype(BF16)
                        s = [jnp.where(f == w, v, old) for f, old in zip(freq, s)]
                    spec[slot, pl.ds((2 * t + c2) * GROUP, GROUP), cols] = jnp.concatenate(s, axis=0)
        for h in range(2):
            copy(h, g).wait()
        cols = pl.ds(g * depth, depth)
        tiles = []
        for c in range(STACK):
            column = []
            for y in range(2):
                line = pl.multiple_of(start_of(y) + g * high + c * rows, 16)
                column += [weight[z, pl.ds(line, rows), :] for z in range(nz)]
            tiles.append(jnp.concatenate(column, axis=0))
        x = jnp.concatenate([mine[:, cols], theirs[:, cols]], axis=0)
        part = lax.dot_general(x, jnp.concatenate(tiles, axis=1), NT, preferred_element_type=F32) * (1.0 - STEP * DECAY)
        part += lax.dot_general(tokens[:, cols], spec[slot], NN, preferred_element_type=F32)
        for p, out in enumerate((own, other)):
            half = part[p * batch : (p + 1) * batch]
            out[...] = half if g == 0 else out[...] + half


def sides_kernel(core, mine, theirs, new_weight):
    half = mine.shape[1]
    new_weight[:, pl.ds(pl.multiple_of(core[0] * half, LANES), half)] = mine[...]
    new_weight[:, pl.ds(pl.multiple_of((1 - core[0]) * half, LANES), half)] = theirs[...]


def swap(x, axis):
    return lax.ppermute(x, axis, [(0, 1), (1, 0)])


def body(sizes, tokens, momentum, gradient, weight, kept_index):
    nx, nyl, nc, nyh, nz = sizes
    rows, width = weight.shape
    half = width // nc
    groups = width // (STACK * LANES)
    units = groups
    deep = -(-units // STACK)
    shards = nyh * nz
    batch = tokens.shape[0]
    pair = basis_pair()
    high = pair.astype(jnp.bfloat16)
    low = (pair - high.astype(np.float32)).astype(jnp.bfloat16)
    core = lax.axis_index("core")

    order = kept_index.reshape(rows, groups, STACK, 2, KEEP).transpose(4, 1, 3, 2, 0).reshape(KEEP * nc * units, LANES)
    smem = pl.BlockSpec(memory_space=pltpu.SMEM)
    vmem = pl.BlockSpec(memory_space=pltpu.VMEM)
    core_ref = core.reshape(1)
    size = half // LANES * rows + KEEP * units
    near = call(
        functools.partial(join_kernel, units),
        jax.ShapeDtypeStruct((size, LANES), BF16),
        (core_ref, weight, order),
        flops=0,
        in_specs=[smem, vmem, vmem],
    )
    last = nyh * nyl - 1
    far = lax.ppermute(near, ("ylo", "yhi"), [(i, last - i) for i in range(last + 1)])
    kept, new_momentum = call(
        functools.partial(local_kernel, nc),
        (
            jax.ShapeDtypeStruct((nc * STACK * KEEP * deep, LANES), F32),
            jax.ShapeDtypeStruct((rows, width), F32),
        ),
        (momentum[0], gradient[0], order, jnp.asarray(pair)),
        flops=0,
        scratch_shapes=[pltpu.VMEM((STACK, deep, nc * KEEP, LANES), F32)],
    )
    far, _ = lax.optimization_barrier((far, kept))
    duo = jnp.concatenate([near, far], axis=0)

    pieces = lax.all_to_all(kept.reshape(nyl * nc * nx, 1, deep * LANES), ("ylo", "core", "x"), 0, 0, tiled=True)
    pieces, _ = lax.optimization_barrier((pieces, duo))
    old_all = lax.all_gather(duo, "z", axis=0, tiled=False)
    lines = STACK * KEEP * deep
    total = to_all(jnp.sum(pieces, axis=0), ("ylo", "x"), nyl * nx).reshape(lines, LANES)
    copies = call(
        functools.partial(pack_kernel, units),
        jax.ShapeDtypeStruct((shards, KEEP * units, LANES), BF16),
        (total,),
        flops=0,
    )
    sums = lax.all_to_all(copies, ("yhi", "z"), 0, 0, tiled=True)

    own_new = call(
        weight_kernel,
        jax.ShapeDtypeStruct((rows, half), BF16),
        (core_ref, total, order, jnp.asarray(np.concatenate([high, high, low], axis=0)), weight),
        flops=0,
        in_specs=[smem, vmem, vmem, vmem, vmem],
        scratch_shapes=[pltpu.VMEM((STACK, KEEP * deep, LANES), F32)],
    )
    other_new = swap(own_new, "core")
    new_weight = call(
        sides_kernel,
        jax.ShapeDtypeStruct((rows, width), BF16),
        (core_ref, own_new, other_new),
        flops=0,
        in_specs=[smem, vmem, vmem],
    )

    mine = lax.dynamic_slice(tokens, (0, core * half), (batch, half))
    theirs = swap(lax.dynamic_slice(tokens, (0, (1 - core) * half), (batch, half)), "core")
    turned = call(
        tokens_kernel,
        jax.ShapeDtypeStruct((nc * batch, half), BF16),
        (mine, theirs, jnp.asarray(high), jnp.asarray(low)),
        flops=0,
    )
    turned, _ = lax.optimization_barrier((turned, other_new))
    out_width = shards * rows
    part = jax.ShapeDtypeStruct((batch, out_width), F32)
    table = pltpu.VMEM((STACK, out_width // LANES, KEEP * units, LANES), F32)
    here, there = call(
        functools.partial(product_kernel, rows, units),
        (part, part),
        (
            lax.axis_index("yhi").reshape(1),
            sums,
            turned,
            mine,
            theirs,
            pltpu.with_memory_space_constraint(old_all, pltpu.HBM),
        ),
        flops=0,
        vmem=20,
        in_specs=[smem, vmem, vmem, vmem, vmem, pl.BlockSpec(memory_space=pltpu.HBM)],
        scratch_shapes=[
            pltpu.VMEM((nz, 2 * size, LANES), BF16),
            table,
            table,
            pltpu.VMEM((2, 2 * STACK * GROUP, out_width), BF16),
            pltpu.SemaphoreType.DMA((2, units // 2 + 1)),
        ],
    )
    projected = (here + swap(there, "core")).astype(BF16)
    return new_weight, new_momentum[None], projected


def run(sizes, devices):
    fine = Mesh(devices.reshape(sizes), AXES)
    rep, fsdp = AXES[:3], AXES[3:]
    return jax.shard_map(
        functools.partial(body, sizes),
        mesh=fine,
        in_specs=(P(AXES, None), P(rep, fsdp, None), P(rep, fsdp, None), P(fsdp, None), P(fsdp, None, None)),
        out_specs=(P(fsdp, None), P(rep, fsdp, None), P(AXES, None)),
        check_vma=False,
    )


def solution(mesh):
    return run((8, 4, 2, 2, 8), mesh.devices)
```
